512 devices in a mesh: dp: 2 (over core), ctx: 32 (over z, x), tp: 8 (over y).
Axes of the slice: x: 4, y: 8, z: 8, core: 2. Of those that a mesh axis runs over, the one named last changes fastest.
Arguments:
- query_rows: bfloat16 [2, 4096, 12288], P('dp', 'ctx', 'tp'), may hold values from -100 to 100
- key_rows: bfloat16 [2, 4096, 1024], P('dp', 'ctx', 'tp'), may hold values from -4 to 4
- value_matrix: bfloat16 [2, 4096, 1024], P('dp', 'ctx', 'tp'), may hold values from -6 to 6
- attention_result: bfloat16 [2, 4096, 12288], P('dp', 'ctx', 'tp'), may hold values from -6 to 6
- loss_output_gradient: bfloat16 [2, 4096, 12288], P('dp', 'ctx', 'tp'), may hold values from -6 to 6
- response_index: int32 [2, 4096], P('dp', 'ctx'), may hold values from 0 to 3, never falling along the last dimension, each value on 1 to 2048 neighbouring positions
- kv_weight: bfloat16 [12288, 2048], P(('dp', 'ctx'), 'tp'), may hold values from -0.0546875 to 0.0546875
Outputs:
- query_grad: bfloat16 [2, 4096, 12288], P('dp', 'ctx', 'tp')
- key_grad: bfloat16 [2, 4096, 1024], P('dp', 'ctx', 'tp')
- value_grad: bfloat16 [2, 4096, 1024], P('dp', 'ctx', 'tp')
- input_grad: bfloat16 [2, 4096, 12288], P('dp', ('ctx', 'tp'))
The draws below stay inside these ranges and needn't reach their ends.
Inputs may be any that keep to these rules, and one draw needn't show every extreme that they name: `response_index`: in each row the numbers never fall; each response holds 1 to 2048 consecutive tokens and one holds exactly 2048.
All inputs are finite; a program needn't handle non-finite values.
Results may differ from the reference program's by a relative error of at most 0.018.
Values may be sent and summed in bfloat16 or wider, within the bound.
A program may use at most 64 MiB of HBM per device.

```python
import math
import jax
import jax.numpy as jnp
import numpy as np
from jax import lax

D = 12288
HEAD_SIZE = 128
QUERY_PER_KEY = 12
KEY_VALUE_HEADS = 8
QUERY_HEADS = 96
PACKED_ROWS = 2
ROW_LENGTH = 4096
MAX_RESPONSE = 2048
RESPONSE_COUNT = 4


def shared_base(key):
    return jax.random.truncated_normal(key, -4.0, 4.0, (PACKED_ROWS, ROW_LENGTH, KEY_VALUE_HEADS, HEAD_SIZE), jnp.float32)


def draw_key_rows(key, part):
    base_offset = shared_base(key)
    return base_offset.reshape(PACKED_ROWS, ROW_LENGTH, KEY_VALUE_HEADS * HEAD_SIZE).astype(jnp.bfloat16)


def draw_query_rows(key, part):
    key = jax.random.fold_in(key, 12)
    query_matrix = jax.random.truncated_normal(key, -4.0, 4.0, (PACKED_ROWS, ROW_LENGTH, KEY_VALUE_HEADS, QUERY_PER_KEY, HEAD_SIZE), jnp.float32)
    return query_matrix.reshape(PACKED_ROWS, ROW_LENGTH, KEY_VALUE_HEADS * QUERY_PER_KEY * HEAD_SIZE).astype(jnp.bfloat16)


def block_levels(own_key, extent, split, smallest, top_value):
    loudness, own = 1.0, jax.random.fold_in(own_key, 6)
    for axis_at, shards_of in split:
        heights = jnp.exp(jax.random.uniform(jax.random.fold_in(own, axis_at), (shards_of,), jnp.float32, smallest / len(split), top_value / len(split)))
        loudness = loudness * jnp.repeat(heights, extent[axis_at] // shards_of).reshape([-1 if axis == axis_at else 1 for axis in range(len(extent))])
    return loudness


def profile(count, total, reach, slope):
    portions = [(1 << 20) // math.isqrt(rank ** slope) + 1 for rank in range(2, count + 1)]
    spare, counts = total - reach - (count - 1), [1] * (count - 1)
    while spare > 0:
        free = [i for i in range(count - 1) if counts[i] < reach]
        mass, left = sum([portions[i] for i in free]), spare
        for i in free:
            extra = min(reach - counts[i], max(1, left * portions[i] // mass), spare)
            counts[i] = counts[i] + extra
            spare = spare - extra
    return np.array([reach] + counts)


def uneven(stream_key, count, total, most, skew):
    if count == 2:
        one = jax.random.randint(stream_key, (), max(1, total - most), min(most, total - 1) + 1)
        return jnp.stack([one, total - one])
    sizes = jnp.asarray(profile(count, total, most, skew), jnp.int32)
    twos = (count - 1) // 2
    giver, sink = sizes[1:1 + 2 * twos:2], sizes[2:2 + 2 * twos:2]
    margin = jnp.minimum(giver - 1, most - sink)
    shifted = jax.random.randint(jax.random.fold_in(stream_key, 1), (twos,), 0, 1 << 20) % (margin + 1)
    sizes = sizes.at[1:1 + 2 * twos:2].set(giver - shifted).at[2:2 + 2 * twos:2].set(sink + shifted)
    return sizes[jax.random.permutation(jax.random.fold_in(stream_key, 2), count)]


def bell_draw(stream_key, dims, spread, bound, split=(), held_as=jnp.bfloat16):
    gain = block_levels(stream_key, dims, split, -0.22, 0.18) if split else 1.0
    drawn = jax.random.normal(stream_key, dims, jnp.float32) * spread * gain
    return jnp.minimum(jnp.maximum(drawn, -bound), bound).astype(held_as)


def setup_inputs(seed: int = 0) -> dict:
    key_of = jax.random.split(jax.random.key(seed), 8)
    query_rows = draw_query_rows(jax.random.fold_in(key_of[7], 71), 0)
    key_rows = draw_key_rows(jax.random.fold_in(key_of[7], 71), 0)
    value_matrix = bell_draw(key_of[2], (PACKED_ROWS, ROW_LENGTH, KEY_VALUE_HEADS * HEAD_SIZE), 1.0, 6.0, ((0, 2), (1, 32), (2, 8)))
    attention_result = bell_draw(key_of[3], (PACKED_ROWS, ROW_LENGTH, QUERY_HEADS * HEAD_SIZE), 1.0, 6.0, ((0, 2), (1, 32), (2, 8)))
    loss_output_gradient = bell_draw(key_of[4], (PACKED_ROWS, ROW_LENGTH, QUERY_HEADS * HEAD_SIZE), 1.0, 6.0, ((0, 2), (1, 32), (2, 8)))
    response_index = jax.vmap(lambda own: jnp.searchsorted(jnp.cumsum(uneven(own, RESPONSE_COUNT, ROW_LENGTH, MAX_RESPONSE, 2)), jnp.arange(ROW_LENGTH), side="right"))(jax.random.split(key_of[5], PACKED_ROWS)).reshape((PACKED_ROWS, ROW_LENGTH)).astype(jnp.int32)
    kv_weight = bell_draw(key_of[6], (D, KEY_VALUE_HEADS * 2 * HEAD_SIZE), D ** -0.5, 0.0546875, ((0, 64), (1, 8)))
    return {"query_rows": query_rows, "key_rows": key_rows, "value_matrix": value_matrix, "attention_result": attention_result, "loss_output_gradient": loss_output_gradient, "response_index": response_index, "kv_weight": kv_weight}


def round_half(values):
    return lax.optimization_barrier(values.astype(jnp.bfloat16)).astype(jnp.float32)


def rotation(positions, width):
    half = width // 2
    inverse = jnp.exp(-jnp.log(1000000.0) * (2.0 * jnp.arange(half, dtype=jnp.float32) / width))
    angle = positions[:, None] * inverse[None, :]
    angle = jnp.concatenate([angle, angle], axis=-1)
    return jnp.cos(angle), jnp.sin(angle)


def unrotate(grad, cosine, sine):
    half = grad.shape[-1] // 2
    turned = jnp.concatenate([-grad[..., half:], grad[..., :half]], axis=-1)
    return grad * cosine - turned * sine


def group_backward(query_matrix, keys, values, outputs, grads_out, segs):
    length = keys.shape[0]
    qblock = min(512, length)
    scale = HEAD_SIZE ** -0.5
    delta = jnp.sum(grads_out.astype(jnp.float32) * outputs.astype(jnp.float32), axis=-1)
    token_places = jnp.arange(length).astype(jnp.int32)
    key_float = keys.astype(jnp.float32)
    value_float = values.astype(jnp.float32)

    def one_block(carry, start):
        key_sum, value_sum = carry
        query_block = lax.dynamic_slice_in_dim(query_matrix, start, qblock, 0).astype(jnp.float32)
        grad_block = lax.dynamic_slice_in_dim(grads_out, start, qblock, 0).astype(jnp.float32)
        delta_block = lax.dynamic_slice_in_dim(delta, start, qblock, 0)
        seg_block = lax.dynamic_slice_in_dim(segs, start, qblock, 0)
        query_pos = start + jnp.arange(qblock).astype(jnp.int32)
        allowed = (seg_block[:, None] == segs[None, :]) & (query_pos[:, None] >= token_places[None, :])
        scores = jnp.einsum('qgd,kd->gqk', query_block, key_float) * scale
        scores = jnp.where(allowed[None], scores, -jnp.inf)
        top = jnp.max(scores, axis=-1, keepdims=True)
        total = jnp.sum(jnp.exp(scores - top), axis=-1, keepdims=True)
        prob = jnp.exp(scores - (top + jnp.log(total)))
        prob_b = round_half(prob)
        value_sum = value_sum + jnp.einsum('gqk,qgd->kd', prob_b, grad_block)
        dprob = jnp.einsum('qgd,kd->gqk', grad_block, value_float)
        dscore = round_half(prob * (dprob - jnp.transpose(delta_block)[:, :, None]))
        query_grad = jnp.einsum('gqk,kd->qgd', dscore, key_float) * scale
        key_sum = key_sum + jnp.einsum('gqk,qgd->kd', dscore, query_block) * scale
        return (key_sum, value_sum), query_grad.astype(jnp.bfloat16)

    starts = (jnp.arange(length // qblock) * qblock).astype(jnp.int32)
    empty = jnp.zeros((length, HEAD_SIZE), jnp.float32)
    (key_sum, value_sum), query_grad = lax.scan(one_block, (empty, empty), starts)
    return query_grad.reshape(length, query_matrix.shape[1], HEAD_SIZE), key_sum, value_sum


def reference(query_rows, key_rows, value_matrix, attention_result, loss_output_gradient, response_index, kv_weight):
    rows, length = response_index.shape
    heads_kv = key_rows.shape[-1] // HEAD_SIZE
    group = query_rows.shape[-1] // (heads_kv * HEAD_SIZE)

    def split_query(values):
        shaped = values.reshape(rows, length, heads_kv, group, HEAD_SIZE).transpose(0, 2, 1, 3, 4)
        return shaped.reshape(rows * heads_kv, length, group, HEAD_SIZE)

    def split_key(values):
        return values.reshape(rows, length, heads_kv, HEAD_SIZE).transpose(0, 2, 1, 3).reshape(rows * heads_kv, length, HEAD_SIZE)

    segs = jnp.repeat(response_index, heads_kv, axis=0)
    pieces = (split_query(query_rows), split_key(key_rows), split_key(value_matrix),
              split_query(attention_result), split_query(loss_output_gradient), segs)
    query_grad, key_sum, value_sum = lax.map(lambda item: group_backward(*item), pieces)
    query_grad = query_grad.reshape(rows, heads_kv, length, group, HEAD_SIZE).transpose(0, 2, 1, 3, 4)
    query_grad = query_grad.reshape(rows, length, heads_kv * group * HEAD_SIZE)

    def join_key(values):
        return values.reshape(rows, heads_kv, length, HEAD_SIZE).transpose(0, 2, 1, 3).reshape(rows, length, heads_kv * HEAD_SIZE)

    value_half = value_sum.astype(jnp.bfloat16)
    key_grad = join_key(key_sum.astype(jnp.bfloat16))
    value_grad = join_key(value_half)
    positions = jnp.arange(length).astype(jnp.float32)
    cosine, sine = rotation(positions, HEAD_SIZE)
    key_pre = unrotate(key_sum, cosine, sine).astype(jnp.bfloat16)
    joined = jnp.concatenate([key_pre, value_half], axis=-1).reshape(rows, heads_kv, length, 2 * HEAD_SIZE)
    joined = joined.transpose(1, 0, 2, 3)
    weight = kv_weight.reshape(kv_weight.shape[0], heads_kv, 2 * HEAD_SIZE).transpose(1, 0, 2)

    def add_head(total, item):
        rows_grad, columns = item
        term = jnp.einsum('rld,nd->rln', rows_grad.astype(jnp.float32), columns.astype(jnp.float32))
        return total + round_half(term), None

    start = jnp.zeros((rows, length, kv_weight.shape[0]), jnp.float32)
    total, _ = lax.scan(add_head, start, (joined, weight))
    return query_grad, key_grad, value_grad, total.astype(jnp.bfloat16)
```

```python
import functools
import jax
import jax.numpy as jnp
import numpy as np
from jax import lax
from jax.experimental import pallas as pl
from jax.experimental.pallas import tpu as pltpu
from jax.sharding import PartitionSpec as P

HEAD = 128
TOK = 128
NX = 4
REACH = 4
LOG2E = 1.4426950408889634
NEG = -1e30
MESH = pl.DeviceIdType.MESH
NT = (((1,), (1,)), ((), ()))
NN = (((1,), (0,)), ((), ()))
f32 = jnp.float32
bf16 = jnp.bfloat16


def dot(a, b, dims):
    return lax.dot_general(a, b, dims, preferred_element_type=f32)


def kernel(
    nc, nz, nx, ny, group, rb,
    q_ref, k_ref, v_ref, o_ref, do_ref, lab_ref, w_ref, inv_ref,
    dq_ref, dk_ref, dv_ref, dx_ref,
    qs, dos, kbuf, vbuf, kt, labown, labs, sbuf, bias, mrow, lrow, frow, dqt, acc,
    outbox, own32, rx, zout, rz, gloc, gy, gall, obuf, oin, wf, ssem, rsem,
):
    c = lax.axis_index("dp")
    ctx = lax.axis_index("ctx")
    y = lax.axis_index("tp")
    z, x = lax.div(ctx, nx), lax.rem(ctx, nx)
    scale = HEAD ** (-0.5)
    planes = REACH + 1
    keys = nx * TOK
    piece = TOK // ny
    count = [0]
    sends = []

    def at_z(d):
        return {"ctx": lax.rem(z + d + nz, nz) * nx + x}

    def at_x(d):
        return {"ctx": z * nx + lax.rem(x + d, nx)}

    def at_y(d):
        return {"tp": lax.rem(y + d + ny, ny)}

    def send(src, dst, device):
        n = count[0]
        count[0] = n + 1
        copy = pltpu.make_async_remote_copy(
            src_ref=src, dst_ref=dst, send_sem=ssem.at[n], recv_sem=rsem.at[n],
            device_id=device, device_id_type=MESH,
        )
        copy.start()
        sends.append(copy)
        return copy

    def rows(i, n):
        return pl.ds(pl.multiple_of(i * n, n), n)

    sibling = {"dp": 1 - c}
    peers = [at_z(d) for d in range(1, nz)] + [at_x(d) for d in range(1, nx)]
    peers += [at_y(d) for d in range(1, ny)] + ([sibling] if nc == 2 else [])
    barrier = pltpu.get_barrier_semaphore()
    for peer in peers:
        pl.semaphore_signal(barrier, inc=1, device_id=peer, device_id_type=MESH)
    pl.semaphore_wait(barrier, len(peers))

    mine = rows(x, TOK)
    own_lab = lab_ref[...]
    labown[...] = jnp.broadcast_to(own_lab, (8, TOK))
    labs[x, 0] = jnp.broadcast_to(own_lab, (8, TOK))
    lab_z = [send(labown, labs.at[x, s], at_z(s)) for s in range(1, planes)]
    kz = [None] + [send(k_ref.at[0], kbuf.at[s, mine], at_z(s)) for s in range(1, planes)]
    kx = {0: [send(k_ref.at[0], kbuf.at[0, mine], at_x(d)) for d in range(1, nx)]}
    vz = [None] + [send(v_ref.at[0], vbuf.at[s, mine], at_z(s)) for s in range(1, planes)]
    vx = {0: [send(v_ref.at[0], vbuf.at[0, mine], at_x(d)) for d in range(1, nx)]}
    wx = [send(w_ref, wf.at[y, c, x], at_x(d)) for d in range(1, nx)]
    kbuf[0, mine] = k_ref[0]
    vbuf[0, mine] = v_ref[0]
    wf[y, c, x] = w_ref[...]

    lane = lax.broadcasted_iota(jnp.int32, (TOK, HEAD), 1)
    for h in range(group):
        cols = slice(h * HEAD, (h + 1) * HEAD)
        part = slice(h * TOK, (h + 1) * TOK)
        qs[part, :] = q_ref[0, :, cols]
        grad = do_ref[0, :, cols]
        dos[part, 0:HEAD] = grad
        delta = -jnp.sum(
            grad.astype(f32) * o_ref[0, :, cols].astype(f32), axis=1, keepdims=True
        )
        high = delta.astype(bf16).astype(f32)
        middle = (delta - high).astype(bf16).astype(f32)
        low = delta - high - middle
        extra = jnp.where(lane == 0, high, jnp.where(lane == 1, middle, low))
        dos[part, HEAD:] = jnp.where(lane < 3, extra, 0.0).astype(bf16)

    dqt[...] = jnp.zeros_like(dqt)

    for copy in lab_z:
        copy.wait_recv()
    lab_x = [send(labs.at[x], labs.at[x], at_x(d)) for d in range(1, nx)]
    for copy in lab_x:
        copy.wait_recv()
    start = jnp.zeros((1, TOK), f32)
    for value in range(1, 4):
        tally = jnp.zeros((8, TOK), f32)
        for s in range(planes):
            here = jnp.zeros((8, TOK), f32)
            for other in range(nx):
                here += jnp.where(labs[other, s] < value, 1.0, 0.0)
            tally += here * jnp.where(z >= s, 1.0, 0.0)
        total = jnp.sum(tally, axis=1, keepdims=True)[0:1]
        start = jnp.where(own_lab == value, total, start)
    start = start + (jnp.maximum(z - REACH, 0) * keys).astype(f32)
    lane1 = lax.broadcasted_iota(jnp.int32, (1, TOK), 1)
    query_at = (lane1 + ctx * TOK).astype(f32)

    width = 2 * TOK
    chunks = group * TOK // width

    def pass_one(s):
        plane = lax.rem(z - s + nz, nz)
        key_at = (lax.broadcasted_iota(jnp.int32, (keys, TOK), 0) + plane * keys).astype(f32)
        allowed = (key_at >= start) & (key_at <= query_at)
        bias[...] = jnp.where(allowed, 0.0, NEG)

        def body(i, carry):
            part = rows(i, width)
            scores = dot(kbuf[s], qs[part, :], NT) * (scale * LOG2E)
            more = bias[...]
            scores = scores + jnp.concatenate([more, more], axis=1)
            top = jnp.max(scores, axis=0, keepdims=True)
            e = jnp.exp2(scores - top)
            sbuf[s, i] = e
            mrow[s : s + 1, part] = top
            lrow[s : s + 1, part] = jnp.sum(e, axis=0, keepdims=True)
            return carry

        lax.fori_loop(0, chunks, body, 0)

    wsteps = []

    def w_begin():
        for copy in wx:
            copy.wait_recv()
        up = send(wf.at[y, c], wf.at[y, c], at_y(1))
        down = send(wf.at[y, c], wf.at[y, c], at_y(-1))
        over = send(wf.at[y, c], wf.at[y, c], sibling) if nc == 2 else None
        wsteps.append((up, down, over))

    half = ny // 2

    def w_step(k):
        up, down, _ = wsteps[-1]
        from_up = lax.rem(y - k + ny, ny)
        from_down = lax.rem(y + k, ny)
        last = nx // 2
        up.wait_recv()
        new_up = new_down = None
        if k + 1 < half:
            new_up = send(wf.at[from_up, c], wf.at[from_up, c], at_y(1))
        elif k + 1 == half:
            new_up = send(
                wf.at[from_up, c, 0:last], wf.at[from_up, c, 0:last], at_y(1)
            )
        overs = []
        if down is not None:
            down.wait_recv()
        if k + 1 < half:
            new_down = send(wf.at[from_down, c], wf.at[from_down, c], at_y(-1))
        elif k + 1 == half:
            new_down = send(
                wf.at[from_down, c, last:nx], wf.at[from_down, c, last:nx], at_y(-1)
            )
        if nc == 2:
            overs.append(send(wf.at[from_up, c], wf.at[from_up, c], sibling))
            if k < half:
                overs.append(send(wf.at[from_down, c], wf.at[from_down, c], sibling))
        wsteps.append((new_up, new_down, overs))

    for s in range(planes):
        if s < REACH:
            kz[s + 1].wait_recv()
            kx[s + 1] = [
                send(kbuf.at[s + 1, mine], kbuf.at[s + 1, mine], at_x(d)) for d in range(1, nx)
            ]
        if s > 0:
            vz[s].wait_recv()
            vx[s] = [send(vbuf.at[s, mine], vbuf.at[s, mine], at_x(d)) for d in range(1, nx)]
        for copy in kx[s]:
            copy.wait_recv()
        pass_one(s)
        if s == 0:
            w_begin()

    top = jnp.max(mrow[0:planes, :], axis=0, keepdims=True)
    shift = mrow[0:planes, :] - top
    total = jnp.sum(lrow[0:planes, :] * jnp.exp2(shift), axis=0, keepdims=True)
    frow[0:planes, :] = jnp.exp2(shift - jnp.log2(total))

    ones = jnp.where(
        lax.broadcasted_iota(jnp.int32, (keys, HEAD), 1) < 3, 1.0, 0.0
    ).astype(bf16)

    def pass_two(s):
        kt[...] = kbuf[s].astype(f32).T.astype(bf16)
        acc[...] = jnp.zeros_like(acc)

        def body(i, carry):
            part = rows(i, width)
            prob = sbuf[s, i] * frow[s : s + 1, part]
            grads = dos[part, :]
            dprob = dot(jnp.concatenate([vbuf[s], ones], axis=1), grads, NT)
            dscore = (prob * dprob).astype(bf16)
            acc[:, HEAD:] += dot(prob.astype(bf16), grads[:, 0:HEAD], NN)
            acc[:, 0:HEAD] += dot(dscore, qs[part, :], NN)
            dqt[:, part] += dot(kt[...], dscore, NN)
            return carry

        lax.fori_loop(0, chunks, body, 0)
        acc[:, 0:HEAD] = acc[:, 0:HEAD] * scale
        for other in range(nx):
            outbox[s, other] = acc[other * TOK : (other + 1) * TOK, :].astype(bf16)
        own32[s] = acc[mine, :]

    def summed(s):
        total = own32[s]
        for copy in back_x[s]:
            copy.wait_recv()
        for d in range(nx - 1):
            total = total + rx[s, d].astype(f32)
        return total

    back_x, back_z = {}, []
    for s in range(REACH, -1, -1):
        for copy in vx[s]:
            copy.wait_recv()
        pass_two(s)
        back_x[s] = [
            send(outbox.at[s, lax.rem(x + d, nx)], rx.at[s, d - 1], at_x(d))
            for d in range(1, nx)
        ]
        if s < REACH:
            zout[s] = summed(s + 1).astype(bf16)
            back_z.append(send(zout.at[s], rz.at[s], at_z(-(s + 1))))
        if s == REACH - 1:
            w_step(1)
        if s == 1:
            w_step(2)

    for h in range(group):
        cols = slice(h * HEAD, (h + 1) * HEAD)
        dq_ref[0, :, cols] = (dqt[:, cols].T * scale).astype(bf16)

    row_at = (lax.broadcasted_iota(jnp.int32, (TOK, HEAD), 0) + ctx * TOK).astype(f32)
    angle = row_at * inv_ref[...]
    cosine, sine = jnp.cos(angle), jnp.sin(angle)

    total = summed(0)
    for copy in back_z:
        copy.wait_recv()
    for s in range(REACH):
        total = total + rz[s].astype(f32)
    key_sum = total[:, 0:HEAD]
    value_half = total[:, HEAD:].astype(bf16)
    dk_ref[0] = key_sum.astype(bf16)
    dv_ref[0] = value_half
    turned = pltpu.roll(key_sum, HEAD // 2, axis=1)
    turned = jnp.where(lane < HEAD // 2, -turned, turned)
    gloc[:, 0:HEAD] = (key_sum * cosine - turned * sine).astype(bf16)
    gloc[:, HEAD:] = value_half

    gy_in = [
        send(gloc.at[rows(lax.rem(y + d, ny), piece)], gy.at[y], at_y(d)) for d in range(1, ny)
    ]
    gy[y] = gloc[rows(y, piece), :]
    for copy in gy_in:
        copy.wait_recv()
    g_in = [send(gy, gall.at[z], at_z(d)) for d in range(1, nz)]
    gall[z] = gy[...]
    for k in range(3, half + 1):
        w_step(k)
    if nc == 2:
        wsteps[0][2].wait_recv()
        for _, _, overs in wsteps[1:]:
            for copy in overs:
                copy.wait_recv()
    for copy in g_in:
        copy.wait_recv()

    cols_each = nx * rb
    for core in range(nc):
        part = jnp.zeros((nz * piece, cols_each), f32)
        for h in range(ny):
            tokens = gall[:, h].reshape(nz * piece, 2 * HEAD)
            part = part + dot(tokens, wf[h, core].reshape(cols_each, 2 * HEAD), NT)
        obuf[:, :, core * cols_each : (core + 1) * cols_each] = part.astype(bf16).reshape(
            nz, piece, cols_each
        )
    o_in = [send(obuf.at[lax.rem(z + d, nz)], oin.at[z], at_z(d)) for d in range(1, nz)]
    oin[z] = obuf[z]
    for copy in o_in:
        copy.wait_recv()
    for core in range(nc):
        for m in range(nz):
            at = (core * nz + m) * cols_each
            dx_ref[0, :, at : at + cols_each] = oin[
                m, :, core * cols_each : (core + 1) * cols_each
            ]
    for copy in sends:
        copy.wait_send()


def local(sizes, q, k, v, o, do, lab, w):
    nc, nz, nx, ny = sizes
    group = q.shape[-1] // HEAD
    rb = w.shape[0]
    planes, keys, piece = REACH + 1, nx * TOK, TOK // ny
    d_all = rb * nc * nz * nx
    half = HEAD // 2
    inv = np.exp(
        -np.log(np.float32(1000000.0)) * (np.float32(2.0) * np.arange(half, dtype=np.float32) / HEAD)
    ).astype(np.float32)
    inv = jnp.asarray(np.concatenate([inv, inv])[None, :])
    copies = 160
    vm = pltpu.VMEM
    scratch = [
        vm((group * TOK, HEAD), bf16),
        vm((group * TOK, 2 * HEAD), bf16),
        vm((planes, keys, HEAD), bf16),
        vm((planes, keys, HEAD), bf16),
        vm((HEAD, keys), bf16),
        vm((8, TOK), jnp.int32),
        vm((nx, planes, 8, TOK), jnp.int32),
        vm((planes, group // 2, keys, 2 * TOK), f32),
        vm((keys, TOK), f32),
        vm((8, group * TOK), f32),
        vm((8, group * TOK), f32),
        vm((8, group * TOK), f32),
        vm((HEAD, group * TOK), f32),
        vm((keys, 2 * HEAD), f32),
        vm((planes, nx, TOK, 2 * HEAD), bf16),
        vm((planes, TOK, 2 * HEAD), f32),
        vm((planes, nx - 1, TOK, 2 * HEAD), bf16),
        vm((REACH, TOK, 2 * HEAD), bf16),
        vm((REACH, TOK, 2 * HEAD), bf16),
        vm((TOK, 2 * HEAD), bf16),
        vm((ny, piece, 2 * HEAD), bf16),
        vm((nz, ny, piece, 2 * HEAD), bf16),
        vm((nz, piece, nc * nx * rb), bf16),
        vm((nz, piece, nc * nx * rb), bf16),
        vm((ny, nc, nx, rb, 2 * HEAD), bf16),
        pltpu.SemaphoreType.DMA((copies,)),
        pltpu.SemaphoreType.DMA((copies,)),
    ]
    spec = pl.BlockSpec(memory_space=pltpu.VMEM)
    return pl.pallas_call(
        functools.partial(kernel, nc, nz, nx, ny, group, rb),
        out_shape=(
            jax.ShapeDtypeStruct(q.shape, bf16),
            jax.ShapeDtypeStruct(k.shape, bf16),
            jax.ShapeDtypeStruct(v.shape, bf16),
            jax.ShapeDtypeStruct((1, piece, d_all), bf16),
        ),
        in_specs=[spec] * 8,
        out_specs=(spec,) * 4,
        scratch_shapes=scratch,
        compiler_params=pltpu.CompilerParams(
            collective_id=0, has_side_effects=True, vmem_limit_bytes=56 * 1024 * 1024
        ),
    )(q, k, v, o, do, lab, w, inv)


def solution(mesh):
    nx = NX
    sizes = (mesh.shape["dp"], mesh.shape["ctx"] // nx, nx, mesh.shape["tp"])
    in_specs = (
        P("dp", "ctx", "tp"),
        P("dp", "ctx", "tp"),
        P("dp", "ctx", "tp"),
        P("dp", "ctx", "tp"),
        P("dp", "ctx", "tp"),
        P("dp", "ctx"),
        P(("dp", "ctx"), "tp"),
    )
    out_specs = (
        P("dp", "ctx", "tp"),
        P("dp", "ctx", "tp"),
        P("dp", "ctx", "tp"),
        P("dp", ("ctx", "tp"), None),
    )
    return jax.shard_map(
        functools.partial(local, sizes),
        mesh=mesh, in_specs=in_specs, out_specs=out_specs, check_vma=False,
    )
```

```python
import functools
import jax
import jax.numpy as jnp
import numpy as np
from jax import lax
from jax.experimental import pallas as pl
from jax.experimental.pallas import tpu as pltpu
from jax.sharding import PartitionSpec as P

HEAD = 128
TOK = 128
NX = 4
REACH = 4
PACK = TOK + 16
LOG2E = 1.4426950408889634
NEG = -1e30
MESH = pl.DeviceIdType.MESH
NT = (((1,), (1,)), ((), ()))
NN = (((1,), (0,)), ((), ()))
f32 = jnp.float32
bf16 = jnp.bfloat16


def dot(a, b, dims):
    return lax.dot_general(a, b, dims, preferred_element_type=f32)


class Semaphores:
    def __init__(self):
        self.used = 0

    def take(self, count):
        first = self.used
        self.used += count
        return first


def kernel(
    nc, nz, nx, ny, group, rb,
    lab_ref, inv_ref, q_ref, k_ref, v_ref, o_ref, do_ref, w_ref,
    dq_ref, dk_ref, dv_ref, dx_ref,
    qin, oin0, doin, qs, dos, kbuf, vbuf, kt, sbuf, bias, mrow, lrow, frow, dqt, acc,
    outbox, own32, rx, zout, rz, gloc, gy, gall, obuf, oin, wf,
    dq_out, dk_out, dv_out, dx_out, ssem, rsem, lsem,
):
    c = lax.axis_index("dp")
    ctx = lax.axis_index("ctx")
    y = lax.axis_index("tp")
    z, x = lax.div(ctx, nx), lax.rem(ctx, nx)
    scale = HEAD ** (-0.5)
    planes = REACH + 1
    keys = nx * TOK
    piece = TOK // ny
    wide = group * TOK
    half = ny // 2
    slots = nz // 2
    sems = Semaphores()
    ends = []

    def at(dz, dx):
        return {"ctx": lax.rem(z + dz + nz, nz) * nx + lax.rem(x + dx, nx)}

    def at_y(d):
        return {"tp": lax.rem(y + d + ny, ny)}

    sibling = {"dp": 1 - c}
    odd = lax.rem(z, 2)
    other_z = 1 - 2 * odd
    members = [(dp, dx) for dp in range(2) for dx in range(nx) if dp + dx > 0]
    me = odd * nx + x

    def at_member(dp, dx):
        return at(dp * other_z, dx)

    def member(dp, dx):
        return lax.rem(odd + dp, 2) * nx + lax.rem(x + dx, nx)

    def remote(n, src, dst, device):
        return pltpu.make_async_remote_copy(
            src_ref=src, dst_ref=dst, send_sem=ssem.at[n], recv_sem=rsem.at[n],
            device_id=device, device_id_type=MESH,
        )

    def send(n, src, dst, device):
        remote(n, src, dst, device).start()

    def arrived(n, dst):
        remote(n, dst, dst, at_y(1)).wait_recv()

    def sent(n, src):
        remote(n, src, src, at_y(1)).wait_send()

    peers = [at(d, 0) for d in range(1, nz)] + [at(0, d) for d in range(1, nx)]
    peers += [at_member(1, dx) for dx in range(1, nx)]
    peers += [at_y(d) for d in range(1, ny)] + ([sibling] if nc == 2 else [])
    barrier = pltpu.get_barrier_semaphore()
    for peer in peers:
        pl.semaphore_signal(barrier, inc=1, device_id=peer, device_id_type=MESH)

    mine = pl.ds(pl.multiple_of(x * TOK, TOK), TOK)
    zslot = lax.div(z, 2)
    local_in = [
        pltpu.make_async_copy(src, dst, lsem.at[n])
        for n, (src, dst) in enumerate([
            (k_ref.at[0], kbuf.at[0, x, 0:TOK]),
            (v_ref.at[0], vbuf.at[0, mine]),
            (do_ref.at[0], doin),
            (o_ref.at[0], oin0),
            (q_ref.at[0], qin),
            (w_ref, wf.at[y, c, zslot]),
        ])
    ]
    for copy in local_in:
        copy.start()
    own_lab = lab_ref[...].astype(f32)
    kbuf[0, x, TOK:PACK] = jnp.broadcast_to(own_lab, (PACK - TOK, TOK)).astype(bf16)
    local_in[0].wait()
    local_in[1].wait()
    pl.semaphore_wait(barrier, len(peers))

    n_kz, n_vz = sems.take(planes), sems.take(planes)
    n_kx, n_vx = sems.take(planes * (nx - 1)), sems.take(planes * (nx - 1))

    def keys_x(s):
        for d in range(1, nx):
            send(n_kx + s * (nx - 1) + d - 1, kbuf.at[s, x], kbuf.at[s, x], at(0, d))

    def values_x(s):
        for d in range(1, nx):
            send(n_vx + s * (nx - 1) + d - 1, vbuf.at[s, mine], vbuf.at[s, mine], at(0, d))

    keys_x(0)
    for s in range(1, planes):
        send(n_kz + s, kbuf.at[0, x], kbuf.at[s, x], at(s, 0))
    wz = [(sems.take(1), d) for d in range(2, nz, 2)]
    for n, d in wz:
        send(n, w_ref, wf.at[y, c, zslot], at(d, 0))
    values_x(0)
    for s in range(1, planes):
        send(n_vz + s, vbuf.at[0, mine], vbuf.at[s, mine], at(s, 0))

    for copy in local_in[2:]:
        copy.wait()
    lane = lax.broadcasted_iota(jnp.int32, (TOK, HEAD), 1)
    for h in range(group):
        cols = slice(h * HEAD, (h + 1) * HEAD)
        part = slice(h * TOK, (h + 1) * TOK)
        qs[part, :] = qin[:, cols]
        grad = doin[:, cols]
        dos[part, 0:HEAD] = grad
        delta = -jnp.sum(
            grad.astype(f32) * oin0[:, cols].astype(f32), axis=1, keepdims=True
        )
        high = delta.astype(bf16).astype(f32)
        middle = (delta - high).astype(bf16).astype(f32)
        low = delta - high - middle
        extra = jnp.where(lane == 0, high, jnp.where(lane == 1, middle, low))
        dos[part, HEAD:] = jnp.where(lane < 3, extra, 0.0).astype(bf16)

    dqt[...] = jnp.zeros_like(dqt)
    row = lax.broadcasted_iota(jnp.int32, (TOK, TOK), 0)
    query_at = lane + ctx * TOK

    n_up, n_down, n_over = sems.take(half + 1), sems.take(half + 1), sems.take(2 * half + 2)
    split = slots // 2

    def ring_refs(d):
        low, high = lax.rem(y - d + ny, ny), lax.rem(y + d, ny)
        if d < half:
            return wf.at[low, c], wf.at[high, c]
        return wf.at[low, c, 0:split], wf.at[high, c, split:slots]

    def w_begin():
        for n, _ in wz:
            arrived(n, wf.at[y, c, 0])
        send(n_up + 1, wf.at[y, c], wf.at[y, c], at_y(1))
        send(n_down + 1, wf.at[y, c], wf.at[y, c], at_y(-1))
        if nc == 2:
            send(n_over, wf.at[y, c], wf.at[y, c], sibling)

    def w_step(d):
        low, high = ring_refs(d)
        arrived(n_up + d, low)
        if d < half:
            part = low if d + 1 < half else wf.at[lax.rem(y - d + ny, ny), c, 0:split]
            send(n_up + d + 1, part, part, at_y(1))
        arrived(n_down + d, high)
        if d < half:
            part = high if d + 1 < half else wf.at[lax.rem(y + d, ny), c, split:slots]
            send(n_down + d + 1, part, part, at_y(-1))
        if nc == 2:
            send(n_over + 2 * d, low, low, sibling)
            send(n_over + 2 * d + 1, high, high, sibling)

    def pass_one(s, carry):
        @pl.when(s < REACH)
        def _():
            arrived(n_kz + s + 1, kbuf.at[0, x])
            keys_x(s + 1)

        @pl.when(s > 0)
        def _():
            arrived(n_vz + s, vbuf.at[0, mine])
            values_x(s)

        for d in range(nx - 1):
            arrived(n_kx + s * (nx - 1) + d, kbuf.at[0, x])
        plane = lax.rem(z - s + nz, nz)
        for other in range(nx):
            labels = kbuf[s, other, TOK:PACK].astype(f32)[0:1]
            labels = jnp.broadcast_to(labels, (TOK, TOK)).T
            key_at = row + (plane * nx + other) * TOK
            allowed = (labels == own_lab) & (key_at <= query_at)
            bias[other * TOK : (other + 1) * TOK, :] = jnp.where(allowed, 0.0, NEG)
        block = jnp.concatenate([kbuf[s, other, 0:TOK] for other in range(nx)], axis=0)
        width = 2 * TOK
        for i in range(wide // width):
            part = slice(i * width, (i + 1) * width)
            scores = dot(block, qs[part, :], NT) * (scale * LOG2E)
            more = bias[...]
            scores = scores + jnp.concatenate([more, more], axis=1)
            top = jnp.max(scores, axis=0, keepdims=True)
            e = jnp.exp2(scores - top)
            sbuf[s, :, part] = e
            mrow[s, :, part] = top
            lrow[s, :, part] = jnp.sum(e, axis=0, keepdims=True)

        @pl.when(s == 1)
        def _():
            w_begin()

        return carry

    lax.fori_loop(0, planes, pass_one, 0)

    top = mrow[0]
    for s in range(1, planes):
        top = jnp.maximum(top, mrow[s])
    total = jnp.zeros_like(top)
    for s in range(planes):
        total = total + lrow[s] * jnp.exp2(mrow[s] - top)
    lse = top + jnp.log2(total)
    for s in range(planes):
        frow[s] = jnp.exp2(mrow[s] - lse)

    ones = jnp.where(
        lax.broadcasted_iota(jnp.int32, (keys, HEAD), 1) < 3, 1.0, 0.0
    ).astype(bf16)
    n_bx, n_bz = sems.take(planes * (nx - 1)), sems.take(planes)

    def summed(s):
        for d in range(nx - 1):
            arrived(n_bx + s * (nx - 1) + d, rx.at[0, 0])
        total = own32[s]
        for d in range(nx - 1):
            total = total + rx[s, d].astype(f32)
        return total

    def pass_two(r, carry):
        s = REACH - r
        for d in range(nx - 1):
            arrived(n_vx + s * (nx - 1) + d, vbuf.at[0, mine])
        block = jnp.concatenate([kbuf[s, other, 0:TOK] for other in range(nx)], axis=0)
        kt[...] = block.astype(f32).T.astype(bf16)
        prob = sbuf[s] * frow[s]
        dprob = dot(jnp.concatenate([vbuf[s], ones], axis=1), dos[...], NT)
        dscore = (prob * dprob).astype(bf16)
        acc[:, HEAD:] = dot(prob.astype(bf16), dos[:, 0:HEAD], NN)
        acc[:, 0:HEAD] = dot(dscore, qs[...], NN) * scale
        dqt[...] += dot(kt[...], dscore, NN)
        for other in range(nx):
            outbox[s, other] = acc[other * TOK : (other + 1) * TOK, :].astype(bf16)
        own32[s] = acc[mine, :]
        for d in range(1, nx):
            send(
                n_bx + s * (nx - 1) + d - 1,
                outbox.at[s, lax.rem(x + d, nx)], rx.at[s, d - 1], at(0, d),
            )

        @pl.when(s < REACH)
        def _():
            zout[s] = summed(s + 1).astype(bf16)
            send(n_bz + s, zout.at[s], rz.at[s], at(-(s + 1), 0))

        for d in range(1, half - 1):
            @pl.when(s == half - 2 - d)
            def _(d=d):
                w_step(d)

        return carry

    lax.fori_loop(0, planes, pass_two, 0)

    for h in range(group):
        cols = slice(h * HEAD, (h + 1) * HEAD)
        dq_out[0, :, cols] = (dqt[:, cols].T * scale).astype(bf16)
    local_out = [pltpu.make_async_copy(dq_out, dq_ref, lsem.at[6])]
    local_out[0].start()

    row_at = (row + ctx * TOK).astype(f32)
    angle = row_at * inv_ref[...]
    cosine, sine = jnp.cos(angle), jnp.sin(angle)

    total = summed(0)
    for s in range(REACH):
        arrived(n_bz + s, rz.at[0])
        total = total + rz[s].astype(f32)
    key_sum = total[:, 0:HEAD]
    value_half = total[:, HEAD:].astype(bf16)
    turned = pltpu.roll(key_sum, HEAD // 2, axis=1)
    turned = jnp.where(lane < HEAD // 2, -turned, turned)
    gloc[:, 0:HEAD] = (key_sum * cosine - turned * sine).astype(bf16)
    gloc[:, HEAD:] = value_half

    n_gy, n_g, n_o = sems.take(ny), sems.take(len(members)), sems.take(len(members))

    def tokens_of(d):
        return gloc.at[pl.ds(pl.multiple_of(lax.rem(y + d, ny) * piece, piece), piece)]

    for d in range(1, ny):
        send(n_gy + d, tokens_of(d), gy.at[y], at_y(d))
    gy[y] = gloc[pl.ds(pl.multiple_of(y * piece, piece), piece), :]
    dk_out[0] = key_sum.astype(bf16)
    dv_out[0] = value_half
    local_out.append(pltpu.make_async_copy(dk_out, dk_ref, lsem.at[7]))
    local_out.append(pltpu.make_async_copy(dv_out, dv_ref, lsem.at[8]))
    local_out[1].start()
    local_out[2].start()
    w_step(half - 1)
    for d in range(1, ny):
        arrived(n_gy + d, gy.at[0])

    for n, (dp, dx) in enumerate(members):
        send(n_g + n, gy, gall.at[me], at_member(dp, dx))
    gall[me] = gy[...]
    w_step(half)
    if nc == 2:
        arrived(n_over, wf.at[0, 0])
        for d in range(1, half + 1):
            low, high = ring_refs(d)
            arrived(n_over + 2 * d, low)
            arrived(n_over + 2 * d + 1, high)
    for n in range(len(members)):
        arrived(n_g + n, gy)

    count = 2 * nx
    tokens = jnp.concatenate(
        [gall[:, h].reshape(count * piece, 2 * HEAD) for h in range(ny)], axis=1
    )
    side = lax.rem(x, 2)
    whole = pl.ds(pl.multiple_of(side * (HEAD // 2), HEAD // 2), HEAD)
    rest = pl.ds(pl.multiple_of((1 - side) * HEAD, HEAD // 2), HEAD // 2)

    def weight_rows(n, rows):
        core, j = n // slots, n % slots
        return jnp.concatenate([wf[h, core, j, rows, :] for h in range(ny)], axis=1)

    shares = nc * slots
    for n in range(0, shares, 2):
        block = jnp.concatenate([weight_rows(n, whole), weight_rows(n + 1, whole)], axis=0)
        part = dot(tokens, block, NT).astype(bf16)
        obuf[:, :, n * HEAD : (n + 2) * HEAD] = part.reshape(count, piece, 2 * HEAD)
    for n in range(0, shares, 4):
        block = []
        for m in (n, n + 2):
            core, j = m // slots, m % slots
            first = jnp.concatenate([wf[h, core, j + side, rest, :] for h in range(ny)], axis=1)
            second = jnp.concatenate(
                [wf[h, core, j + 1 - side, rest, :] for h in range(ny)], axis=1
            )
            block += [first, second]
        part = dot(tokens, jnp.concatenate(block, axis=0), NT).astype(bf16)
        base = shares * HEAD + n * (HEAD // 2)
        obuf[:, :, base : base + 2 * HEAD] = part.reshape(count, piece, 2 * HEAD)

    for n, (dp, dx) in enumerate(members):
        send(n_o + n, obuf.at[member(dp, dx)], oin.at[me], at_member(dp, dx))
    oin[me] = obuf[me]
    for n in range(len(members)):
        arrived(n_o + n, oin.at[0])
    left = lax.broadcasted_iota(jnp.int32, (piece, HEAD), 1) < HEAD // 2
    for p in range(2):
        for e in range(nx // 2):
            even, uneven = p * nx + 2 * e, p * nx + 2 * e + 1
            for n in range(shares):
                core, j = n // slots, n % slots
                first = core * (nz * nx * rb) + (2 * j + p) * nx * rb + e * 2 * rb
                dx_out[0, :, first : first + HEAD] = oin[even, :, n * HEAD : (n + 1) * HEAD]
                dx_out[0, :, first + 2 * HEAD : first + 3 * HEAD] = oin[
                    uneven, :, n * HEAD : (n + 1) * HEAD
                ]
                base = shares * HEAD + n // 2 * HEAD
                a = oin[even, :, base : base + HEAD].astype(f32)
                b = oin[uneven, :, base : base + HEAD].astype(f32)
                if n % 2 == 0:
                    middle = jnp.where(left, a, b)
                else:
                    middle = pltpu.roll(jnp.where(left, b, a), HEAD // 2, axis=1)
                dx_out[0, :, first + HEAD : first + 2 * HEAD] = middle.astype(bf16)
    local_out.append(pltpu.make_async_copy(dx_out, dx_ref, lsem.at[9]))
    local_out[3].start()

    for s in range(planes):
        for d in range(nx - 1):
            sent(n_kx + s * (nx - 1) + d, kbuf.at[0, x])
            sent(n_vx + s * (nx - 1) + d, vbuf.at[0, mine])
            sent(n_bx + s * (nx - 1) + d, rx.at[0, 0])
        if s > 0:
            sent(n_kz + s, kbuf.at[0, x])
            sent(n_vz + s, vbuf.at[0, mine])
            sent(n_bz + s - 1, rz.at[0])
    for n, _ in wz:
        sent(n, w_ref)
    for d in range(1, half + 1):
        low, high = ring_refs(d)
        sent(n_up + d, low)
        sent(n_down + d, high)
        if nc == 2:
            sent(n_over + 2 * d, low)
            sent(n_over + 2 * d + 1, high)
    if nc == 2:
        sent(n_over, wf.at[0, 0])
    for d in range(1, ny):
        sent(n_gy + d, gy.at[0])
    for n in range(len(members)):
        sent(n_g + n, gy)
        sent(n_o + n, oin.at[0])
    for copy in local_out:
        copy.wait()


def hand_out(*refs):
    count = len(refs) // 2
    copies = [
        pltpu.make_async_copy(refs[n], refs[count + n], refs[-1].at[n]) for n in range(count)
    ]
    for copy in copies:
        copy.start()
    for copy in copies:
        copy.wait()


def local(sizes, q, k, v, o, do, lab, w):
    nc, nz, nx, ny = sizes
    group = q.shape[-1] // HEAD
    rb = w.shape[0]
    planes, keys, piece = REACH + 1, nx * TOK, TOK // ny
    d_all = rb * nc * nz * nx
    half = HEAD // 2
    inv = np.exp(
        -np.log(np.float32(1000000.0)) * (np.float32(2.0) * np.arange(half, dtype=np.float32) / HEAD)
    ).astype(np.float32)
    inv = jnp.asarray(np.concatenate([inv, inv])[None, :])
    copies = 160
    vm = pltpu.VMEM
    wide = group * TOK
    share = nc * (nz // 2) * rb
    scratch = [
        vm((TOK, wide), bf16),
        vm((TOK, wide), bf16),
        vm((TOK, wide), bf16),
        vm((wide, HEAD), bf16),
        vm((wide, 2 * HEAD), bf16),
        vm((planes, nx, PACK, HEAD), bf16),
        vm((planes, keys, HEAD), bf16),
        vm((HEAD, keys), bf16),
        vm((planes, keys, wide), f32),
        vm((keys, TOK), f32),
        vm((planes, 1, wide), f32),
        vm((planes, 1, wide), f32),
        vm((planes, 1, wide), f32),
        vm((HEAD, wide), f32),
        vm((keys, 2 * HEAD), f32),
        vm((planes, nx, TOK, 2 * HEAD), bf16),
        vm((planes, TOK, 2 * HEAD), f32),
        vm((planes, nx - 1, TOK, 2 * HEAD), bf16),
        vm((REACH, TOK, 2 * HEAD), bf16),
        vm((REACH, TOK, 2 * HEAD), bf16),
        vm((TOK, 2 * HEAD), bf16),
        vm((ny, piece, 2 * HEAD), bf16),
        vm((2 * nx, ny, piece, 2 * HEAD), bf16),
        vm((2 * nx, piece, share), bf16),
        vm((2 * nx, piece, share), bf16),
        vm((ny, nc, nz // 2, rb, 2 * HEAD), bf16),
        vm(q.shape, bf16),
        vm(k.shape, bf16),
        vm(v.shape, bf16),
        vm((1, piece, d_all), bf16),
        pltpu.SemaphoreType.DMA((copies,)),
        pltpu.SemaphoreType.DMA((copies,)),
        pltpu.SemaphoreType.DMA((10,)),
    ]
    spec = pl.BlockSpec(memory_space=pltpu.VMEM)
    far = pl.BlockSpec(memory_space=pltpu.HBM)
    results = tuple(
        jax.ShapeDtypeStruct(shape, bf16)
        for shape in (q.shape, k.shape, v.shape, (1, piece, d_all))
    )
    out = pl.pallas_call(
        functools.partial(kernel, nc, nz, nx, ny, group, rb),
        out_shape=results,
        in_specs=[spec] * 2 + [far] * 6,
        out_specs=(far,) * 4,
        scratch_shapes=scratch,
        compiler_params=pltpu.CompilerParams(
            collective_id=0, has_side_effects=True, vmem_limit_bytes=60 * 1024 * 1024
        ),
    )(lab, inv, q, k, v, o, do, w)
    return pl.pallas_call(
        hand_out,
        out_shape=results,
        in_specs=[far] * 4,
        out_specs=(far,) * 4,
        scratch_shapes=[pltpu.SemaphoreType.DMA((4,))],
    )(*out)


def solution(mesh):
    nx = NX
    sizes = (mesh.shape["dp"], mesh.shape["ctx"] // nx, nx, mesh.shape["tp"])
    in_specs = (
        P("dp", "ctx", "tp"),
        P("dp", "ctx", "tp"),
        P("dp", "ctx", "tp"),
        P("dp", "ctx", "tp"),
        P("dp", "ctx", "tp"),
        P("dp", "ctx"),
        P(("dp", "ctx"), "tp"),
    )
    out_specs = (
        P("dp", "ctx", "tp"),
        P("dp", "ctx", "tp"),
        P("dp", "ctx", "tp"),
        P("dp", ("ctx", "tp"), None),
    )
    return jax.shard_map(
        functools.partial(local, sizes),
        mesh=mesh, in_specs=in_specs, out_specs=out_specs, check_vma=False,
    )
```

```python
import functools
import jax
import jax.numpy as jnp
import numpy as np
from jax import lax
from jax.experimental import pallas as pl
from jax.experimental.pallas import tpu as pltpu
from jax.sharding import PartitionSpec as P

HEAD = 128
TOK = 128
NX = 4
REACH = 4
PACK = TOK + 16
LOG2E = 1.4426950408889634
NEG = -1e30
MESH = pl.DeviceIdType.MESH
NT = (((1,), (1,)), ((), ()))
NN = (((1,), (0,)), ((), ()))
f32 = jnp.float32
bf16 = jnp.bfloat16


def dot(a, b, dims):
    return lax.dot_general(a, b, dims, preferred_element_type=f32)


class Semaphores:
    def __init__(self):
        self.used = 0

    def take(self, count):
        first = self.used
        self.used += count
        return first


def kernel(
    nc, nz, nx, ny, group, rb,
    lab_ref, inv_ref, q_ref, k_ref, v_ref, o_ref, do_ref, w_ref,
    dq_ref, dk_ref, dv_ref, dx_ref,
    qin, oin0, doin, qs, dos, kbuf, vbuf, kt, sbuf, bias, mrow, lrow, frow, dqt, acc,
    outbox, own32, rx, zout, rz, gloc, gy, gall, obuf, oin, wf, krelay, vrelay,
    dq_out, dk_out, dv_out, dx_out, ssem, rsem, lsem,
):
    c = lax.axis_index("dp")
    ctx = lax.axis_index("ctx")
    y = lax.axis_index("tp")
    z, x = lax.div(ctx, nx), lax.rem(ctx, nx)
    scale = HEAD ** (-0.5)
    planes = REACH + 1
    keys = nx * TOK
    piece = TOK // ny
    wide = group * TOK
    half = ny // 2
    slots = nz // 2
    sems = Semaphores()
    ends = []

    def at(dz, dx):
        return {"ctx": lax.rem(z + dz + nz, nz) * nx + lax.rem(x + dx, nx)}

    def at_y(d):
        return {"tp": lax.rem(y + d + ny, ny)}

    sibling = {"dp": 1 - c}
    odd = lax.rem(z, 2)
    other_z = 1 - 2 * odd
    members = [(dp, dx) for dp in range(2) for dx in range(nx) if dp + dx > 0]
    me = odd * nx + x

    def at_member(dp, dx):
        return at(dp * other_z, dx)

    def member(dp, dx):
        return lax.rem(odd + dp, 2) * nx + lax.rem(x + dx, nx)

    def remote(n, src, dst, device):
        return pltpu.make_async_remote_copy(
            src_ref=src, dst_ref=dst, send_sem=ssem.at[n], recv_sem=rsem.at[n],
            device_id=device, device_id_type=MESH,
        )

    def send(n, src, dst, device):
        remote(n, src, dst, device).start()

    def arrived(n, dst):
        remote(n, dst, dst, at_y(1)).wait_recv()

    def sent(n, src):
        remote(n, src, src, at_y(1)).wait_send()

    peers = [at(d, 0) for d in range(1, nz)] + [at(0, d) for d in range(1, nx)]
    peers += [at_member(1, dx) for dx in range(1, nx)]
    peers += [at_y(d) for d in range(1, ny)] + ([sibling] if nc == 2 else [])
    barrier = pltpu.get_barrier_semaphore()
    for peer in peers:
        pl.semaphore_signal(barrier, inc=1, device_id=peer, device_id_type=MESH)

    mine = pl.ds(pl.multiple_of(x * TOK, TOK), TOK)
    local_in = [
        pltpu.make_async_copy(src, dst, lsem.at[n])
        for n, (src, dst) in enumerate([
            (k_ref.at[0], kbuf.at[0, x, 0:TOK]),
            (v_ref.at[0], vbuf.at[0, mine]),
            (do_ref.at[0], doin),
            (o_ref.at[0], oin0),
            (q_ref.at[0], qin),
            (w_ref, wf.at[y, c, lax.div(z, 2)]),
        ])
    ]
    for copy in local_in:
        copy.start()
    own_lab = lab_ref[...].astype(f32)
    kbuf[0, x, TOK:PACK] = jnp.broadcast_to(own_lab, (PACK - TOK, TOK)).astype(bf16)
    local_in[0].wait()
    local_in[1].wait()
    pl.semaphore_wait(barrier, len(peers))

    n_kz, n_vz = sems.take(planes), sems.take(planes)
    n_kx, n_vx = sems.take(planes * (nx - 1)), sems.take(planes * (nx - 1))

    def keys_x(s):
        for d in range(1, nx):
            send(n_kx + s * (nx - 1) + d - 1, kbuf.at[s, x], kbuf.at[s, x], at(0, d))

    def values_x(s):
        for d in range(1, nx):
            send(n_vx + s * (nx - 1) + d - 1, vbuf.at[s, mine], vbuf.at[s, mine], at(0, d))

    n_kr, n_vr = sems.take(1), sems.take(1)
    keys_x(0)
    for s in range(1, REACH):
        send(n_kz + s, kbuf.at[0, x], kbuf.at[s, x], at(s, 0))
    send(n_kr, kbuf.at[0, x], krelay, at(-2, 0))

    far = [0, 2, -2, 4]
    n_w = sems.take(4)
    n_up, n_down = sems.take(4 * (half + 1)), sems.take(4 * (half + 1))
    n_over = sems.take(4 * (2 * half + 1))

    def share(head, k):
        return wf.at[head, c, lax.div(lax.rem(z + far[k] + nz, nz), 2)]

    def low(d):
        return lax.rem(y - d + ny, ny)

    def high(d):
        return lax.rem(y + d, ny)

    def over(k, d, up):
        return n_over + k * (2 * half + 1) + 2 * d - up

    def goes_up(k, d):
        return d < half or (d == half and k < 2)

    def goes_down(k, d):
        return d < half or (d == half and k >= 2)

    def w_start(k, source=None):
        source = share(y, k) if source is None else source
        send(n_up + k * (half + 1) + 1, source, share(y, k), at_y(1))
        send(n_down + k * (half + 1) + 1, source, share(y, k), at_y(-1))
        if nc == 2:
            send(over(k, 0, 0), source, share(y, k), sibling)

    passed = set()

    def w_pass(k, d):
        if (k, d) in passed:
            return
        passed.add((k, d))
        if goes_up(k, d):
            arrived(n_up + k * (half + 1) + d, share(low(d), k))
            if goes_up(k, d + 1):
                send(n_up + k * (half + 1) + d + 1, share(low(d), k), share(low(d), k), at_y(1))
            if nc == 2:
                send(over(k, d, 1), share(low(d), k), share(low(d), k), sibling)
        if goes_down(k, d):
            arrived(n_down + k * (half + 1) + d, share(high(d), k))
            if goes_down(k, d + 1):
                send(n_down + k * (half + 1) + d + 1, share(high(d), k), share(high(d), k), at_y(-1))
            if nc == 2:
                send(over(k, d, 0), share(high(d), k), share(high(d), k), sibling)

    send(n_w + 2, w_ref, share(y, 0), at(2, 0))
    send(n_w + 1, w_ref, share(y, 0), at(-2, 0))
    w_start(0, w_ref)

    for copy in local_in[2:]:
        copy.wait()
    lane = lax.broadcasted_iota(jnp.int32, (TOK, HEAD), 1)
    for h in range(group):
        cols = slice(h * HEAD, (h + 1) * HEAD)
        part = slice(h * TOK, (h + 1) * TOK)
        qs[part, :] = qin[:, cols]
        grad = doin[:, cols]
        dos[part, 0:HEAD] = grad
        delta = -jnp.sum(
            grad.astype(f32) * oin0[:, cols].astype(f32), axis=1, keepdims=True
        )
        first = delta.astype(bf16).astype(f32)
        second = (delta - first).astype(bf16).astype(f32)
        third = delta - first - second
        extra = jnp.where(lane == 0, first, jnp.where(lane == 1, second, third))
        dos[part, HEAD:] = jnp.where(lane < 3, extra, 0.0).astype(bf16)

    dqt[...] = jnp.zeros_like(dqt)
    row = lax.broadcasted_iota(jnp.int32, (TOK, TOK), 0)
    query_at = lane + ctx * TOK

    arrived(n_kr, krelay)
    send(n_kz + REACH, krelay, kbuf.at[REACH, x], at(-2, 0))
    values_x(0)
    for s in range(1, REACH):
        send(n_vz + s, vbuf.at[0, mine], vbuf.at[s, mine], at(s, 0))
    send(n_vr, vbuf.at[0, mine], vrelay, at(-2, 0))

    def pass_one(s, carry):
        @pl.when(s < REACH)
        def _():
            arrived(n_kz + s + 1, kbuf.at[0, x])
            keys_x(s + 1)

        @pl.when(s > 1)
        def _():
            arrived(n_vz + s - 1, vbuf.at[0, mine])
            values_x(s - 1)

        @pl.when(s == 1)
        def _():
            w_pass(0, 1)
            arrived(n_w + 1, w_ref)
            send(n_w + 3, share(y, 1), share(y, 1), at(-2, 0))
            w_start(1)
            arrived(n_w + 2, w_ref)
            w_start(2)

        @pl.when(s == 2)
        def _():
            arrived(n_vr, vrelay)
            send(n_vz + REACH, vrelay, vbuf.at[REACH, mine], at(-2, 0))

        @pl.when(s == REACH)
        def _():
            arrived(n_w + 3, w_ref)
            w_start(3)

        for d in range(nx - 1):
            arrived(n_kx + s * (nx - 1) + d, kbuf.at[0, x])
        plane = lax.rem(z - s + nz, nz)
        for other in range(nx):
            labels = kbuf[s, other, TOK:PACK].astype(f32)[0:1]
            labels = jnp.broadcast_to(labels, (TOK, TOK)).T
            key_at = row + (plane * nx + other) * TOK
            allowed = (labels == own_lab) & (key_at <= query_at)
            bias[other * TOK : (other + 1) * TOK, :] = jnp.where(allowed, 0.0, NEG)
        block = jnp.concatenate([kbuf[s, other, 0:TOK] for other in range(nx)], axis=0)
        width = 2 * TOK
        for i in range(wide // width):
            part = slice(i * width, (i + 1) * width)
            scores = dot(block, qs[part, :], NT) * (scale * LOG2E)
            more = bias[...]
            scores = scores + jnp.concatenate([more, more], axis=1)
            top = jnp.max(scores, axis=0, keepdims=True)
            e = jnp.exp2(scores - top)
            sbuf[s, :, part] = e
            mrow[s, :, part] = top
            lrow[s, :, part] = jnp.sum(e, axis=0, keepdims=True)

        return carry

    lax.fori_loop(0, planes, pass_one, 0)

    arrived(n_vz + REACH, vbuf.at[0, mine])
    values_x(REACH)
    w_pass(0, 2)
    w_pass(1, 1)
    w_pass(2, 1)

    top = mrow[0]
    for s in range(1, planes):
        top = jnp.maximum(top, mrow[s])
    total = jnp.zeros_like(top)
    for s in range(planes):
        total = total + lrow[s] * jnp.exp2(mrow[s] - top)
    lse = top + jnp.log2(total)
    for s in range(planes):
        frow[s] = jnp.exp2(mrow[s] - lse)

    ones = jnp.where(
        lax.broadcasted_iota(jnp.int32, (keys, HEAD), 1) < 3, 1.0, 0.0
    ).astype(bf16)
    n_bx, n_bz = sems.take(planes * (nx - 1)), sems.take(planes)

    def summed(s):
        for d in range(nx - 1):
            arrived(n_bx + s * (nx - 1) + d, rx.at[0, 0])
        total = own32[s]
        for d in range(nx - 1):
            total = total + rx[s, d].astype(f32)
        return total

    def plane_at(r):
        first = (REACH + 1 - r) // 3
        return first * (r + 2) + (1 - first) * (REACH - r)

    def back(s):
        zout[s] = summed(s).astype(bf16)
        send(n_bz + s, zout.at[s], rz.at[s], at(-s, 0))

    def pass_two(r, carry):
        s = plane_at(r)
        for d in range(nx - 1):
            arrived(n_vx + s * (nx - 1) + d, vbuf.at[0, mine])
        block = jnp.concatenate([kbuf[s, other, 0:TOK] for other in range(nx)], axis=0)
        kt[...] = block.astype(f32).T.astype(bf16)
        prob = sbuf[s] * frow[s]
        dprob = dot(jnp.concatenate([vbuf[s], ones], axis=1), dos[...], NT)
        dscore = (prob * dprob).astype(bf16)
        acc[:, HEAD:] = dot(prob.astype(bf16), dos[:, 0:HEAD], NN)
        acc[:, 0:HEAD] = dot(dscore, qs[...], NN) * scale
        dqt[...] += dot(kt[...], dscore, NN)
        for other in range(nx):
            outbox[s, other] = acc[other * TOK : (other + 1) * TOK, :].astype(bf16)
        own32[s] = acc[mine, :]
        for d in range(1, nx):
            send(
                n_bx + s * (nx - 1) + d - 1,
                outbox.at[s, lax.rem(x + d, nx)], rx.at[s, d - 1], at(0, d),
            )

        @pl.when(r >= 2)
        def _():
            back(plane_at(r - 2))

        @pl.when(r == 1)
        def _():
            w_pass(3, 1)

        @pl.when(r == 3)
        def _():
            w_pass(0, 3)
            w_pass(1, 2)
            w_pass(2, 2)

        @pl.when(r == REACH)
        def _():
            w_pass(3, 2)

        return carry

    lax.fori_loop(0, planes, pass_two, 0)

    back(1)

    for h in range(group):
        cols = slice(h * HEAD, (h + 1) * HEAD)
        dq_out[0, :, cols] = (dqt[:, cols].T * scale).astype(bf16)
    local_out = [pltpu.make_async_copy(dq_out, dq_ref, lsem.at[6])]
    local_out[0].start()

    row_at = (row + ctx * TOK).astype(f32)
    angle = row_at * inv_ref[...]
    cosine, sine = jnp.cos(angle), jnp.sin(angle)

    total = summed(0)
    for s in range(1, planes):
        arrived(n_bz + s, rz.at[0])
        total = total + rz[s].astype(f32)
    key_sum = total[:, 0:HEAD]
    value_half = total[:, HEAD:].astype(bf16)
    turned = pltpu.roll(key_sum, HEAD // 2, axis=1)
    turned = jnp.where(lane < HEAD // 2, -turned, turned)
    gloc[:, 0:HEAD] = (key_sum * cosine - turned * sine).astype(bf16)
    gloc[:, HEAD:] = value_half

    n_gy, n_g, n_o = sems.take(ny), sems.take(len(members)), sems.take(len(members))

    def tokens_of(d):
        return gloc.at[pl.ds(pl.multiple_of(lax.rem(y + d, ny) * piece, piece), piece)]

    for d in range(1, ny):
        send(n_gy + d, tokens_of(d), gy.at[y], at_y(d))
    gy[y] = gloc[pl.ds(pl.multiple_of(y * piece, piece), piece), :]
    dk_out[0] = key_sum.astype(bf16)
    dv_out[0] = value_half
    local_out.append(pltpu.make_async_copy(dk_out, dk_ref, lsem.at[7]))
    local_out.append(pltpu.make_async_copy(dv_out, dv_ref, lsem.at[8]))
    local_out[1].start()
    local_out[2].start()
    for k in range(4):
        w_pass(k, 4 if k == 0 else 3)
    for d in range(1, ny):
        arrived(n_gy + d, gy.at[0])

    for n, (dp, dx) in enumerate(members):
        send(n_g + n, gy, gall.at[me], at_member(dp, dx))
    gall[me] = gy[...]
    for k in range(1, 4):
        w_pass(k, half)
    if nc == 2:
        for k in range(4):
            arrived(over(k, 0, 0), w_ref)
            for d in range(1, half + 1):
                if goes_up(k, d):
                    arrived(over(k, d, 1), w_ref)
                if goes_down(k, d):
                    arrived(over(k, d, 0), w_ref)
    for n in range(len(members)):
        arrived(n_g + n, gy)

    count = 2 * nx
    tokens = jnp.concatenate(
        [gall[:, h].reshape(count * piece, 2 * HEAD) for h in range(ny)], axis=1
    )
    side = lax.rem(x, 2)
    whole = pl.ds(pl.multiple_of(side * (HEAD // 2), HEAD // 2), HEAD)
    rest = pl.ds(pl.multiple_of((1 - side) * HEAD, HEAD // 2), HEAD // 2)

    def weight_rows(n, rows):
        core, j = n // slots, n % slots
        return jnp.concatenate([wf[h, core, j, rows, :] for h in range(ny)], axis=1)

    shares = nc * slots
    for n in range(0, shares, 2):
        block = jnp.concatenate([weight_rows(n, whole), weight_rows(n + 1, whole)], axis=0)
        part = dot(tokens, block, NT).astype(bf16)
        obuf[:, :, n * HEAD : (n + 2) * HEAD] = part.reshape(count, piece, 2 * HEAD)
    for n in range(0, shares, 4):
        block = []
        for m in (n, n + 2):
            core, j = m // slots, m % slots
            first = jnp.concatenate([wf[h, core, j + side, rest, :] for h in range(ny)], axis=1)
            second = jnp.concatenate(
                [wf[h, core, j + 1 - side, rest, :] for h in range(ny)], axis=1
            )
            block += [first, second]
        part = dot(tokens, jnp.concatenate(block, axis=0), NT).astype(bf16)
        base = shares * HEAD + n * (HEAD // 2)
        obuf[:, :, base : base + 2 * HEAD] = part.reshape(count, piece, 2 * HEAD)

    for n, (dp, dx) in enumerate(members):
        send(n_o + n, obuf.at[member(dp, dx)], oin.at[me], at_member(dp, dx))
    oin[me] = obuf[me]
    for n in range(len(members)):
        arrived(n_o + n, oin.at[0])
    left = lax.broadcasted_iota(jnp.int32, (piece, HEAD), 1) < HEAD // 2
    for p in range(2):
        for e in range(nx // 2):
            even, uneven = p * nx + 2 * e, p * nx + 2 * e + 1
            for n in range(shares):
                core, j = n // slots, n % slots
                first = core * (nz * nx * rb) + (2 * j + p) * nx * rb + e * 2 * rb
                dx_out[0, :, first : first + HEAD] = oin[even, :, n * HEAD : (n + 1) * HEAD]
                dx_out[0, :, first + 2 * HEAD : first + 3 * HEAD] = oin[
                    uneven, :, n * HEAD : (n + 1) * HEAD
                ]
                base = shares * HEAD + n // 2 * HEAD
                a = oin[even, :, base : base + HEAD].astype(f32)
                b = oin[uneven, :, base : base + HEAD].astype(f32)
                if n % 2 == 0:
                    middle = jnp.where(left, a, b)
                else:
                    middle = pltpu.roll(jnp.where(left, b, a), HEAD // 2, axis=1)
                dx_out[0, :, first + HEAD : first + 2 * HEAD] = middle.astype(bf16)
    local_out.append(pltpu.make_async_copy(dx_out, dx_ref, lsem.at[9]))
    local_out[3].start()

    for s in range(planes):
        for d in range(nx - 1):
            sent(n_kx + s * (nx - 1) + d, kbuf.at[0, x])
            sent(n_vx + s * (nx - 1) + d, vbuf.at[0, mine])
            sent(n_bx + s * (nx - 1) + d, rx.at[0, 0])
        if s > 0:
            sent(n_kz + s, kbuf.at[0, x])
            sent(n_vz + s, vbuf.at[0, mine])
            sent(n_bz + s, rz.at[0])
    sent(n_kr, krelay)
    sent(n_vr, vrelay)
    for k in range(4):
        if k > 0:
            sent(n_w + k, w_ref)
        for d in range(1, half + 1):
            if goes_up(k, d):
                sent(n_up + k * (half + 1) + d, w_ref)
            if goes_down(k, d):
                sent(n_down + k * (half + 1) + d, w_ref)
            if nc == 2 and goes_up(k, d):
                sent(over(k, d, 1), w_ref)
            if nc == 2 and goes_down(k, d):
                sent(over(k, d, 0), w_ref)
        if nc == 2:
            sent(over(k, 0, 0), w_ref)
    for d in range(1, ny):
        sent(n_gy + d, gy.at[0])
    for n in range(len(members)):
        sent(n_g + n, gy)
        sent(n_o + n, oin.at[0])
    for copy in local_out:
        copy.wait()


def hand_out(*refs):
    count = len(refs) // 3
    sources, targets, held, sem = refs[:count], refs[count : 2 * count], refs[2 * count : -1], refs[-1]
    into = [pltpu.make_async_copy(sources[n], held[n], sem.at[n]) for n in range(count)]
    out = [pltpu.make_async_copy(held[n], targets[n], sem.at[count + n]) for n in range(count)]
    for copy in into:
        copy.start()
    for n in range(count):
        into[n].wait()
        out[n].start()
    for copy in out:
        copy.wait()


def local(sizes, q, k, v, o, do, lab, w):
    nc, nz, nx, ny = sizes
    group = q.shape[-1] // HEAD
    rb = w.shape[0]
    planes, keys, piece = REACH + 1, nx * TOK, TOK // ny
    d_all = rb * nc * nz * nx
    half = HEAD // 2
    inv = np.exp(
        -np.log(np.float32(1000000.0)) * (np.float32(2.0) * np.arange(half, dtype=np.float32) / HEAD)
    ).astype(np.float32)
    inv = jnp.asarray(np.concatenate([inv, inv])[None, :])
    copies = 200
    vm = pltpu.VMEM
    wide = group * TOK
    share = nc * (nz // 2) * rb
    scratch = [
        vm((TOK, wide), bf16),
        vm((TOK, wide), bf16),
        vm((TOK, wide), bf16),
        vm((wide, HEAD), bf16),
        vm((wide, 2 * HEAD), bf16),
        vm((planes, nx, PACK, HEAD), bf16),
        vm((planes, keys, HEAD), bf16),
        vm((HEAD, keys), bf16),
        vm((planes, keys, wide), f32),
        vm((keys, TOK), f32),
        vm((planes, 1, wide), f32),
        vm((planes, 1, wide), f32),
        vm((planes, 1, wide), f32),
        vm((HEAD, wide), f32),
        vm((keys, 2 * HEAD), f32),
        vm((planes, nx, TOK, 2 * HEAD), bf16),
        vm((planes, TOK, 2 * HEAD), f32),
        vm((planes, nx - 1, TOK, 2 * HEAD), bf16),
        vm((planes, TOK, 2 * HEAD), bf16),
        vm((planes, TOK, 2 * HEAD), bf16),
        vm((TOK, 2 * HEAD), bf16),
        vm((ny, piece, 2 * HEAD), bf16),
        vm((2 * nx, ny, piece, 2 * HEAD), bf16),
        vm((2 * nx, piece, share), bf16),
        vm((2 * nx, piece, share), bf16),
        vm((ny, nc, nz // 2, rb, 2 * HEAD), bf16),
        vm((PACK, HEAD), bf16),
        vm((TOK, HEAD), bf16),
        vm(q.shape, bf16),
        vm(k.shape, bf16),
        vm(v.shape, bf16),
        vm((1, piece, d_all), bf16),
        pltpu.SemaphoreType.DMA((copies,)),
        pltpu.SemaphoreType.DMA((copies,)),
        pltpu.SemaphoreType.DMA((10,)),
    ]
    spec = pl.BlockSpec(memory_space=pltpu.VMEM)
    far = pl.BlockSpec(memory_space=pltpu.HBM)
    results = tuple(
        jax.ShapeDtypeStruct(shape, bf16)
        for shape in (q.shape, k.shape, v.shape, (1, piece, d_all))
    )
    out = pl.pallas_call(
        functools.partial(kernel, nc, nz, nx, ny, group, rb),
        out_shape=results,
        in_specs=[spec] * 2 + [far] * 6,
        out_specs=(far,) * 4,
        scratch_shapes=scratch,
        compiler_params=pltpu.CompilerParams(
            collective_id=0, has_side_effects=True, vmem_limit_bytes=60 * 1024 * 1024
        ),
    )(lab, inv, q, k, v, o, do, w)
    return pl.pallas_call(
        hand_out,
        out_shape=results,
        in_specs=[far] * 4,
        out_specs=(far,) * 4,
        scratch_shapes=[vm(r.shape, bf16) for r in results] + [pltpu.SemaphoreType.DMA((8,))],
    )(*out)


def solution(mesh):
    nx = NX
    sizes = (mesh.shape["dp"], mesh.shape["ctx"] // nx, nx, mesh.shape["tp"])
    in_specs = (
        P("dp", "ctx", "tp"),
        P("dp", "ctx", "tp"),
        P("dp", "ctx", "tp"),
        P("dp", "ctx", "tp"),
        P("dp", "ctx", "tp"),
        P("dp", "ctx"),
        P(("dp", "ctx"), "tp"),
    )
    out_specs = (
        P("dp", "ctx", "tp"),
        P("dp", "ctx", "tp"),
        P("dp", "ctx", "tp"),
        P("dp", ("ctx", "tp"), None),
    )
    return jax.shard_map(
        functools.partial(local, sizes),
        mesh=mesh, in_specs=in_specs, out_specs=out_specs, check_vma=False,
    )
```

```python
import functools
import jax
import jax.numpy as jnp
import numpy as np
from jax import lax
from jax.experimental import pallas as pl
from jax.experimental.pallas import tpu as pltpu
from jax.sharding import PartitionSpec as P

HEAD = 128
TOK = 128
NX = 4
REACH = 4
PACK = TOK + 16
LOG2E = 1.4426950408889634
NEG = -1e30
MESH = pl.DeviceIdType.MESH
NT = (((1,), (1,)), ((), ()))
NN = (((1,), (0,)), ((), ()))
f32 = jnp.float32
bf16 = jnp.bfloat16


def dot(a, b, dims):
    return lax.dot_general(a, b, dims, preferred_element_type=f32)


class Semaphores:
    def __init__(self):
        self.used = 0

    def take(self, count):
        first = self.used
        self.used += count
        return first


def kernel(
    nc, nz, nx, ny, group, rb,
    lab_ref, inv_ref, q_ref, k_ref, v_ref, o_ref, do_ref, w_ref,
    dq_ref, dk_ref, dv_ref, dx_ref,
    qin, oin0, doin, qs, dos, kbuf, vbuf, kt, sbuf, bias, mrow, lrow, frow, dqt, acc,
    outbox, own32, rx, zout, rz, gloc, gy, gall, obuf, oin, wf, krelay, vrelay,
    dq_out, dk_out, dv_out, dx_out, ssem, rsem, lsem,
):
    c = lax.axis_index("dp")
    ctx = lax.axis_index("ctx")
    y = lax.axis_index("tp")
    z, x = lax.div(ctx, nx), lax.rem(ctx, nx)
    scale = HEAD ** (-0.5)
    planes = REACH + 1
    keys = nx * TOK
    piece = TOK // ny
    wide = group * TOK
    half = ny // 2
    slots = nz // 2
    sems = Semaphores()
    ends = []

    def at(dz, dx):
        return {"ctx": lax.rem(z + dz + nz, nz) * nx + lax.rem(x + dx, nx)}

    def at_y(d):
        return {"tp": lax.rem(y + d + ny, ny)}

    sibling = {"dp": 1 - c}
    odd = lax.rem(z, 2)
    other_z = 1 - 2 * odd
    members = [(dp, dx) for dp in range(2) for dx in range(nx) if dp + dx > 0]
    me = odd * nx + x

    def at_member(dp, dx):
        return at(dp * other_z, dx)

    def member(dp, dx):
        return lax.rem(odd + dp, 2) * nx + lax.rem(x + dx, nx)

    def remote(n, src, dst, device):
        return pltpu.make_async_remote_copy(
            src_ref=src, dst_ref=dst, send_sem=ssem.at[n], recv_sem=rsem.at[n],
            device_id=device, device_id_type=MESH,
        )

    def send(n, src, dst, device):
        remote(n, src, dst, device).start()

    def arrived(n, dst):
        remote(n, dst, dst, at_y(1)).wait_recv()

    def sent(n, src):
        remote(n, src, src, at_y(1)).wait_send()

    peers = [at(d, 0) for d in range(1, nz)] + [at(0, d) for d in range(1, nx)]
    peers += [at_member(1, dx) for dx in range(1, nx)]
    peers += [at_y(d) for d in range(1, ny)] + ([sibling] if nc == 2 else [])
    for s in (0, REACH):
        kbuf[s] = jnp.zeros((nx, PACK, HEAD), bf16)
        vbuf[s] = jnp.zeros((keys, HEAD), bf16)
        rx[s] = jnp.zeros((nx - 1, TOK, 2 * HEAD), bf16)
    barrier = pltpu.get_barrier_semaphore()
    for peer in peers:
        pl.semaphore_signal(barrier, inc=1, device_id=peer, device_id_type=MESH)

    mine = pl.ds(pl.multiple_of(x * TOK, TOK), TOK)
    local_in = [
        pltpu.make_async_copy(src, dst, lsem.at[n])
        for n, (src, dst) in enumerate([
            (k_ref.at[0], kbuf.at[0, x, 0:TOK]),
            (v_ref.at[0], vbuf.at[0, mine]),
            (q_ref.at[0], qin),
            (do_ref.at[0], doin),
            (o_ref.at[0], oin0),
            (w_ref, wf.at[y, c, lax.div(z, 2)]),
        ])
    ]
    for copy in local_in:
        copy.start()
    own_lab = lab_ref[...].astype(f32)
    kbuf[0, x, TOK:PACK] = jnp.broadcast_to(own_lab, (PACK - TOK, TOK)).astype(bf16)
    local_in[0].wait()
    local_in[1].wait()
    pl.semaphore_wait(barrier, len(peers))

    n_kz, n_vz = sems.take(planes), sems.take(planes)
    n_kx, n_vx = sems.take(planes * (nx - 1)), sems.take(planes * (nx - 1))

    def seen(s, key_x, query_x):
        inside = (s > 0) & (s < REACH)
        return inside | ((s == 0) & (key_x < query_x)) | ((s == REACH) & (key_x > query_x))

    def from_x(d):
        return lax.rem(x - d + nx, nx)

    def to_x(d):
        return lax.rem(x + d, nx)

    def keys_x(s):
        for d in range(1, nx):
            @pl.when(seen(s, x, to_x(d)))
            def _(d=d):
                send(n_kx + s * (nx - 1) + d - 1, kbuf.at[s, x], kbuf.at[s, x], at(0, d))

    def values_x(s):
        for d in range(1, nx):
            @pl.when(seen(s, x, to_x(d)))
            def _(d=d):
                send(n_vx + s * (nx - 1) + d - 1, vbuf.at[s, mine], vbuf.at[s, mine], at(0, d))

    n_kr, n_vr = sems.take(1), sems.take(1)
    send(n_kr, kbuf.at[0, x], krelay, at(-2, 0))
    for s in range(1, REACH):
        send(n_kz + s, kbuf.at[0, x], kbuf.at[s, x], at(s, 0))
    keys_x(0)

    far = [0, 2, -2, 4]
    n_w = sems.take(4)
    n_up, n_down = sems.take(4 * (half + 1)), sems.take(4 * (half + 1))
    n_over = sems.take(4 * (2 * half + 1))

    def share(head, k):
        return wf.at[head, c, lax.div(lax.rem(z + far[k] + nz, nz), 2)]

    def low(d):
        return lax.rem(y - d + ny, ny)

    def high(d):
        return lax.rem(y + d, ny)

    def over(k, d, up):
        return n_over + k * (2 * half + 1) + 2 * d - up

    def goes_up(k, d):
        return d < half or (d == half and k < 2)

    def goes_down(k, d):
        return d < half or (d == half and k >= 2)

    def w_start(k, source=None):
        source = share(y, k) if source is None else source
        send(n_up + k * (half + 1) + 1, source, share(y, k), at_y(1))
        send(n_down + k * (half + 1) + 1, source, share(y, k), at_y(-1))
        if nc == 2:
            send(over(k, 0, 0), source, share(y, k), sibling)

    passed = set()

    def w_pass(k, d):
        if (k, d) in passed:
            return
        passed.add((k, d))
        if goes_up(k, d):
            arrived(n_up + k * (half + 1) + d, share(low(d), k))
            if goes_up(k, d + 1):
                send(n_up + k * (half + 1) + d + 1, share(low(d), k), share(low(d), k), at_y(1))
            if nc == 2:
                send(over(k, d, 1), share(low(d), k), share(low(d), k), sibling)
        if goes_down(k, d):
            arrived(n_down + k * (half + 1) + d, share(high(d), k))
            if goes_down(k, d + 1):
                send(n_down + k * (half + 1) + d + 1, share(high(d), k), share(high(d), k), at_y(-1))
            if nc == 2:
                send(over(k, d, 0), share(high(d), k), share(high(d), k), sibling)

    w_start(0, w_ref)

    local_in[2].wait()
    for h in range(group):
        qs[h * TOK : (h + 1) * TOK, :] = qin[:, h * HEAD : (h + 1) * HEAD]

    arrived(n_kr, krelay)
    send(n_kz + REACH, krelay, kbuf.at[REACH, x], at(-2, 0))
    for s in (2, 3, 1):
        send(n_vz + s, vbuf.at[0, mine], vbuf.at[s, mine], at(s, 0))
    send(n_vr, vbuf.at[0, mine], vrelay, at(-2, 0))
    for s in range(1, REACH):
        arrived(n_kz + s, kbuf.at[0, x])
        keys_x(s)
    values_x(0)
    send(n_w + 2, w_ref, share(y, 0), at(2, 0))
    send(n_w + 1, w_ref, share(y, 0), at(-2, 0))

    for copy in local_in[3:]:
        copy.wait()
    lane = lax.broadcasted_iota(jnp.int32, (TOK, HEAD), 1)
    for h in range(group):
        cols = slice(h * HEAD, (h + 1) * HEAD)
        part = slice(h * TOK, (h + 1) * TOK)
        grad = doin[:, cols]
        dos[part, 0:HEAD] = grad
        delta = -jnp.sum(
            grad.astype(f32) * oin0[:, cols].astype(f32), axis=1, keepdims=True
        )
        first = delta.astype(bf16).astype(f32)
        second = (delta - first).astype(bf16).astype(f32)
        third = delta - first - second
        extra = jnp.where(lane == 0, first, jnp.where(lane == 1, second, third))
        dos[part, HEAD:] = jnp.where(lane < 3, extra, 0.0).astype(bf16)

    dqt[...] = jnp.zeros_like(dqt)
    row = lax.broadcasted_iota(jnp.int32, (TOK, TOK), 0)
    query_at = lane + ctx * TOK

    def pass_one(s, carry):
        @pl.when(s == 1)
        def _():
            arrived(n_kz + REACH, kbuf.at[0, x])
            keys_x(REACH)
            arrived(n_vr, vrelay)
            send(n_vz + REACH, vrelay, vbuf.at[REACH, mine], at(-2, 0))
            w_pass(0, 1)

        @pl.when(s == 2)
        def _():
            for n in (2, 3):
                arrived(n_vz + n, vbuf.at[0, mine])
                values_x(n)

        @pl.when(s == REACH)
        def _():
            for n in (REACH, 1):
                arrived(n_vz + n, vbuf.at[0, mine])
                values_x(n)
            arrived(n_w + 1, w_ref)
            send(n_w + 3, share(y, 1), share(y, 1), at(-2, 0))

        for d in range(1, nx):
            @pl.when(seen(s, from_x(d), x))
            def _(d=d):
                arrived(n_kx + s * (nx - 1) + d - 1, kbuf.at[0, x])

        plane = lax.rem(z - s + nz, nz)
        for other in range(nx):
            labels = kbuf[s, other, TOK:PACK].astype(f32)[0:1]
            labels = jnp.broadcast_to(labels, (TOK, TOK)).T
            key_at = row + (plane * nx + other) * TOK
            allowed = (labels == own_lab) & (key_at <= query_at)
            bias[other * TOK : (other + 1) * TOK, :] = jnp.where(allowed, 0.0, NEG)
        block = jnp.concatenate([kbuf[s, other, 0:TOK] for other in range(nx)], axis=0)
        width = 2 * TOK
        for i in range(wide // width):
            part = slice(i * width, (i + 1) * width)
            scores = dot(block, qs[part, :], NT) * (scale * LOG2E)
            more = bias[...]
            scores = scores + jnp.concatenate([more, more], axis=1)
            top = jnp.max(scores, axis=0, keepdims=True)
            e = jnp.exp2(scores - top)
            sbuf[s, :, part] = e
            mrow[s, :, part] = top
            lrow[s, :, part] = jnp.sum(e, axis=0, keepdims=True)

        return carry

    lax.fori_loop(0, planes, pass_one, 0)

    w_pass(0, 2)
    w_start(1)
    arrived(n_w + 2, w_ref)
    w_start(2)

    top = mrow[0]
    for s in range(1, planes):
        top = jnp.maximum(top, mrow[s])
    total = jnp.zeros_like(top)
    for s in range(planes):
        total = total + lrow[s] * jnp.exp2(mrow[s] - top)
    lse = top + jnp.log2(total)
    for s in range(planes):
        frow[s] = jnp.exp2(mrow[s] - lse)

    ones = jnp.where(
        lax.broadcasted_iota(jnp.int32, (keys, HEAD), 1) < 3, 1.0, 0.0
    ).astype(bf16)
    n_bx, n_bz = sems.take(planes * (nx - 1)), sems.take(planes)

    def summed(s):
        for d in range(1, nx):
            @pl.when(seen(s, x, from_x(d)))
            def _(d=d):
                arrived(n_bx + s * (nx - 1) + d - 1, rx.at[0, 0])

        total = own32[s]
        for d in range(nx - 1):
            total = total + rx[s, d].astype(f32)
        return total

    def plane_at(r):
        first = (REACH + 1 - r) // 3
        return first * (r + 2) + (1 - first) * (REACH - r)

    def back(s):
        zout[s] = summed(s).astype(bf16)
        send(n_bz + s, zout.at[s], rz.at[s], at(-s, 0))

    def pass_two(r, carry):
        s = plane_at(r)
        for d in range(1, nx):
            @pl.when(seen(s, from_x(d), x))
            def _(d=d):
                arrived(n_vx + s * (nx - 1) + d - 1, vbuf.at[0, mine])

        block = jnp.concatenate([kbuf[s, other, 0:TOK] for other in range(nx)], axis=0)
        kt[...] = block.astype(f32).T.astype(bf16)
        prob = sbuf[s] * frow[s]
        dprob = dot(jnp.concatenate([vbuf[s], ones], axis=1), dos[...], NT)
        dscore = (prob * dprob).astype(bf16)
        acc[:, HEAD:] = dot(prob.astype(bf16), dos[:, 0:HEAD], NN)
        acc[:, 0:HEAD] = dot(dscore, qs[...], NN) * scale
        dqt[...] += dot(kt[...], dscore, NN)
        for other in range(nx):
            outbox[s, other] = acc[other * TOK : (other + 1) * TOK, :].astype(bf16)
        own32[s] = acc[mine, :]
        for d in range(1, nx):
            @pl.when(seen(s, to_x(d), x))
            def _(d=d):
                send(
                    n_bx + s * (nx - 1) + d - 1,
                    outbox.at[s, to_x(d)], rx.at[s, d - 1], at(0, d),
                )

        @pl.when(r >= 2)
        def _():
            back(plane_at(r - 2))

        @pl.when(r == 1)
        def _():
            arrived(n_w + 3, w_ref)
            w_start(3)

        @pl.when(r == 2)
        def _():
            w_pass(1, 1)
            w_pass(2, 1)
            w_pass(0, 3)

        @pl.when(r == REACH)
        def _():
            w_pass(3, 1)
            w_pass(1, 2)
            w_pass(2, 2)

        return carry

    lax.fori_loop(0, planes, pass_two, 0)

    back(1)

    for h in range(group):
        cols = slice(h * HEAD, (h + 1) * HEAD)
        dq_out[0, :, cols] = (dqt[:, cols].T * scale).astype(bf16)
    local_out = [pltpu.make_async_copy(dq_out, dq_ref, lsem.at[6])]
    local_out[0].start()

    row_at = (row + ctx * TOK).astype(f32)
    angle = row_at * inv_ref[...]
    cosine, sine = jnp.cos(angle), jnp.sin(angle)

    total = summed(0)
    for s in range(1, planes):
        arrived(n_bz + s, rz.at[0])
        total = total + rz[s].astype(f32)
    key_sum = total[:, 0:HEAD]
    value_half = total[:, HEAD:].astype(bf16)
    turned = pltpu.roll(key_sum, HEAD // 2, axis=1)
    turned = jnp.where(lane < HEAD // 2, -turned, turned)
    gloc[:, 0:HEAD] = (key_sum * cosine - turned * sine).astype(bf16)
    gloc[:, HEAD:] = value_half

    n_gy, n_g, n_o = sems.take(ny), sems.take(len(members)), sems.take(2 * len(members))

    def tokens_of(d):
        return gloc.at[pl.ds(pl.multiple_of(lax.rem(y + d, ny) * piece, piece), piece)]

    for d in range(1, ny):
        send(n_gy + d, tokens_of(d), gy.at[y], at_y(d))
    gy[y] = gloc[pl.ds(pl.multiple_of(y * piece, piece), piece), :]
    dk_out[0] = key_sum.astype(bf16)
    dv_out[0] = value_half
    local_out.append(pltpu.make_async_copy(dk_out, dk_ref, lsem.at[7]))
    local_out.append(pltpu.make_async_copy(dv_out, dv_ref, lsem.at[8]))
    local_out[1].start()
    local_out[2].start()
    for k, d in ((0, 4), (3, 2), (1, 3), (2, 3)):
        w_pass(k, d)
    for d in range(1, ny):
        arrived(n_gy + d, gy.at[0])

    for n, (dp, dx) in enumerate(members):
        send(n_g + n, gy, gall.at[me], at_member(dp, dx))
    gall[me] = gy[...]
    w_pass(3, 3)
    for k in range(1, 4):
        w_pass(k, half)
    if nc == 2:
        for k in range(4):
            arrived(over(k, 0, 0), w_ref)
            for d in range(1, half + 1):
                if goes_up(k, d):
                    arrived(over(k, d, 1), w_ref)
                if goes_down(k, d):
                    arrived(over(k, d, 0), w_ref)
    for n in range(len(members)):
        arrived(n_g + n, gy)

    count = 2 * nx
    tokens = jnp.concatenate(
        [gall[:, h].reshape(count * piece, 2 * HEAD) for h in range(ny)], axis=1
    )
    side = lax.rem(x, 2)
    whole = pl.ds(pl.multiple_of(side * (HEAD // 2), HEAD // 2), HEAD)
    rest = pl.ds(pl.multiple_of((1 - side) * HEAD, HEAD // 2), HEAD // 2)

    def weight_rows(n, rows):
        core, j = n // slots, n % slots
        return jnp.concatenate([wf[h, core, j, rows, :] for h in range(ny)], axis=1)

    shares = nc * slots
    for n in range(0, shares, 2):
        block = jnp.concatenate([weight_rows(n, whole), weight_rows(n + 1, whole)], axis=0)
        part = dot(tokens, block, NT).astype(bf16)
        obuf[:, :, n * HEAD : (n + 2) * HEAD] = part.reshape(count, piece, 2 * HEAD)
    front = shares * HEAD
    lots = (pl.ds(0, front), pl.ds(front, front // 2))

    def hand_over(lot):
        for n, (dp, dx) in enumerate(members):
            send(
                n_o + 2 * n + lot, obuf.at[member(dp, dx), :, lots[lot]],
                oin.at[me, :, lots[lot]], at_member(dp, dx),
            )

    hand_over(0)
    for n in range(0, shares, 4):
        block = []
        for m in (n, n + 2):
            core, j = m // slots, m % slots
            first = jnp.concatenate([wf[h, core, j + side, rest, :] for h in range(ny)], axis=1)
            second = jnp.concatenate(
                [wf[h, core, j + 1 - side, rest, :] for h in range(ny)], axis=1
            )
            block += [first, second]
        part = dot(tokens, jnp.concatenate(block, axis=0), NT).astype(bf16)
        base = front + n * (HEAD // 2)
        obuf[:, :, base : base + 2 * HEAD] = part.reshape(count, piece, 2 * HEAD)

    hand_over(1)
    oin[me] = obuf[me]
    for n in range(len(members)):
        arrived(n_o + 2 * n, oin.at[0, :, lots[0]])
        arrived(n_o + 2 * n + 1, oin.at[0, :, lots[1]])
    left = lax.broadcasted_iota(jnp.int32, (piece, HEAD), 1) < HEAD // 2
    for p in range(2):
        for e in range(nx // 2):
            even, uneven = p * nx + 2 * e, p * nx + 2 * e + 1
            for n in range(shares):
                core, j = n // slots, n % slots
                first = core * (nz * nx * rb) + (2 * j + p) * nx * rb + e * 2 * rb
                dx_out[0, :, first : first + HEAD] = oin[even, :, n * HEAD : (n + 1) * HEAD]
                dx_out[0, :, first + 2 * HEAD : first + 3 * HEAD] = oin[
                    uneven, :, n * HEAD : (n + 1) * HEAD
                ]
                base = front + n // 2 * HEAD
                a = oin[even, :, base : base + HEAD].astype(f32)
                b = oin[uneven, :, base : base + HEAD].astype(f32)
                if n % 2 == 0:
                    middle = jnp.where(left, a, b)
                else:
                    middle = pltpu.roll(jnp.where(left, b, a), HEAD // 2, axis=1)
                dx_out[0, :, first + HEAD : first + 2 * HEAD] = middle.astype(bf16)
    local_out.append(pltpu.make_async_copy(dx_out, dx_ref, lsem.at[9]))
    local_out[3].start()

    for s in range(planes):
        for d in range(1, nx):
            @pl.when(seen(s, x, to_x(d)))
            def _(s=s, d=d):
                sent(n_kx + s * (nx - 1) + d - 1, kbuf.at[0, x])
                sent(n_vx + s * (nx - 1) + d - 1, vbuf.at[0, mine])

            @pl.when(seen(s, to_x(d), x))
            def _(s=s, d=d):
                sent(n_bx + s * (nx - 1) + d - 1, rx.at[0, 0])

        if s > 0:
            sent(n_kz + s, kbuf.at[0, x])
            sent(n_vz + s, vbuf.at[0, mine])
            sent(n_bz + s, rz.at[0])
    sent(n_kr, krelay)
    sent(n_vr, vrelay)
    for k in range(4):
        if k > 0:
            sent(n_w + k, w_ref)
        for d in range(1, half + 1):
            if goes_up(k, d):
                sent(n_up + k * (half + 1) + d, w_ref)
            if goes_down(k, d):
                sent(n_down + k * (half + 1) + d, w_ref)
            if nc == 2 and goes_up(k, d):
                sent(over(k, d, 1), w_ref)
            if nc == 2 and goes_down(k, d):
                sent(over(k, d, 0), w_ref)
        if nc == 2:
            sent(over(k, 0, 0), w_ref)
    for d in range(1, ny):
        sent(n_gy + d, gy.at[0])
    for n in range(len(members)):
        sent(n_g + n, gy)
        sent(n_o + 2 * n, oin.at[0, :, lots[0]])
        sent(n_o + 2 * n + 1, oin.at[0, :, lots[1]])
    for copy in local_out:
        copy.wait()


def hand_out(*refs):
    count = len(refs) // 3
    sources, targets, held, sem = refs[:count], refs[count : 2 * count], refs[2 * count : -1], refs[-1]
    into = [pltpu.make_async_copy(sources[n], held[n], sem.at[n]) for n in range(count)]
    out = [pltpu.make_async_copy(held[n], targets[n], sem.at[count + n]) for n in range(count)]
    for copy in into:
        copy.start()
    for n in range(count):
        into[n].wait()
        out[n].start()
    for copy in out:
        copy.wait()


def local(sizes, q, k, v, o, do, lab, w):
    nc, nz, nx, ny = sizes
    group = q.shape[-1] // HEAD
    rb = w.shape[0]
    planes, keys, piece = REACH + 1, nx * TOK, TOK // ny
    d_all = rb * nc * nz * nx
    half = HEAD // 2
    inv = np.exp(
        -np.log(np.float32(1000000.0)) * (np.float32(2.0) * np.arange(half, dtype=np.float32) / HEAD)
    ).astype(np.float32)
    inv = jnp.asarray(np.concatenate([inv, inv])[None, :])
    copies = 200
    vm = pltpu.VMEM
    wide = group * TOK
    share = nc * (nz // 2) * rb
    scratch = [
        vm((TOK, wide), bf16),
        vm((TOK, wide), bf16),
        vm((TOK, wide), bf16),
        vm((wide, HEAD), bf16),
        vm((wide, 2 * HEAD), bf16),
        vm((planes, nx, PACK, HEAD), bf16),
        vm((planes, keys, HEAD), bf16),
        vm((HEAD, keys), bf16),
        vm((planes, keys, wide), f32),
        vm((keys, TOK), f32),
        vm((planes, 1, wide), f32),
        vm((planes, 1, wide), f32),
        vm((planes, 1, wide), f32),
        vm((HEAD, wide), f32),
        vm((keys, 2 * HEAD), f32),
        vm((planes, nx, TOK, 2 * HEAD), bf16),
        vm((planes, TOK, 2 * HEAD), f32),
        vm((planes, nx - 1, TOK, 2 * HEAD), bf16),
        vm((planes, TOK, 2 * HEAD), bf16),
        vm((planes, TOK, 2 * HEAD), bf16),
        vm((TOK, 2 * HEAD), bf16),
        vm((ny, piece, 2 * HEAD), bf16),
        vm((2 * nx, ny, piece, 2 * HEAD), bf16),
        vm((2 * nx, piece, share), bf16),
        vm((2 * nx, piece, share), bf16),
        vm((ny, nc, nz // 2, rb, 2 * HEAD), bf16),
        vm((PACK, HEAD), bf16),
        vm((TOK, HEAD), bf16),
        vm(q.shape, bf16),
        vm(k.shape, bf16),
        vm(v.shape, bf16),
        vm((1, piece, d_all), bf16),
        pltpu.SemaphoreType.DMA((copies,)),
        pltpu.SemaphoreType.DMA((copies,)),
        pltpu.SemaphoreType.DMA((10,)),
    ]
    spec = pl.BlockSpec(memory_space=pltpu.VMEM)
    far = pl.BlockSpec(memory_space=pltpu.HBM)
    results = tuple(
        jax.ShapeDtypeStruct(shape, bf16)
        for shape in (q.shape, k.shape, v.shape, (1, piece, d_all))
    )
    out = pl.pallas_call(
        functools.partial(kernel, nc, nz, nx, ny, group, rb),
        out_shape=results,
        in_specs=[spec] * 2 + [far] * 6,
        out_specs=(far,) * 4,
        scratch_shapes=scratch,
        compiler_params=pltpu.CompilerParams(
            collective_id=0, has_side_effects=True, vmem_limit_bytes=60 * 1024 * 1024
        ),
    )(lab, inv, q, k, v, o, do, w)
    return pl.pallas_call(
        hand_out,
        out_shape=results,
        in_specs=[far] * 4,
        out_specs=(far,) * 4,
        scratch_shapes=[vm(r.shape, bf16) for r in results] + [pltpu.SemaphoreType.DMA((8,))],
    )(*out)


def solution(mesh):
    nx = NX
    sizes = (mesh.shape["dp"], mesh.shape["ctx"] // nx, nx, mesh.shape["tp"])
    in_specs = (
        P("dp", "ctx", "tp"),
        P("dp", "ctx", "tp"),
        P("dp", "ctx", "tp"),
        P("dp", "ctx", "tp"),
        P("dp", "ctx", "tp"),
        P("dp", "ctx"),
        P(("dp", "ctx"), "tp"),
    )
    out_specs = (
        P("dp", "ctx", "tp"),
        P("dp", "ctx", "tp"),
        P("dp", "ctx", "tp"),
        P("dp", ("ctx", "tp"), None),
    )
    return jax.shard_map(
        functools.partial(local, sizes),
        mesh=mesh, in_specs=in_specs, out_specs=out_specs, check_vma=False,
    )
```

```python
import functools
import jax
import jax.numpy as jnp
import numpy as np
from jax import lax
from jax.experimental import pallas as pl
from jax.experimental.pallas import tpu as pltpu
from jax.sharding import PartitionSpec as P

HEAD = 128
TOK = 128
NX = 4
REACH = 4
PACK = TOK + 16
LOG2E = 1.4426950408889634
NEG = -1e30
MESH = pl.DeviceIdType.MESH
NT = (((1,), (1,)), ((), ()))
NN = (((1,), (0,)), ((), ()))
f32 = jnp.float32
bf16 = jnp.bfloat16


def dot(a, b, dims):
    return lax.dot_general(a, b, dims, preferred_element_type=f32)


class Semaphores:
    def __init__(self):
        self.used = 0

    def take(self, count):
        first = self.used
        self.used += count
        return first


def kernel(
    nc, nz, nx, ny, group, rb,
    lab_ref, inv_ref, q_ref, k_ref, v_ref, o_ref, do_ref, w_ref,
    dq_ref, dk_ref, dv_ref, dx_ref,
    qin, oin0, doin, qs, dos, kbuf, vbuf, kt, sbuf, bias, mrow, lrow, frow, dqt, acc,
    outbox, own32, rx, zout, rz, gloc, gy, gall, obuf, oin, wf, krelay, vrelay,
    dq_out, dk_out, dv_out, dx_out, ssem, rsem, lsem,
):
    c = lax.axis_index("dp")
    ctx = lax.axis_index("ctx")
    y = lax.axis_index("tp")
    z, x = lax.div(ctx, nx), lax.rem(ctx, nx)
    scale = HEAD ** (-0.5)
    planes = REACH + 1
    keys = nx * TOK
    piece = TOK // ny
    wide = group * TOK
    half = ny // 2
    slots = nz // 2
    sems = Semaphores()
    ends = []

    def at(dz, dx):
        return {"ctx": lax.rem(z + dz + nz, nz) * nx + lax.rem(x + dx, nx)}

    def at_y(d):
        return {"tp": lax.rem(y + d + ny, ny)}

    sibling = {"dp": 1 - c}
    odd = lax.rem(z, 2)
    other_z = 1 - 2 * odd
    members = [(dp, dx) for dp in range(2) for dx in range(nx) if dp + dx > 0]
    me = odd * nx + x

    def at_member(dp, dx):
        return at(dp * other_z, dx)

    def member(dp, dx):
        return lax.rem(odd + dp, 2) * nx + lax.rem(x + dx, nx)

    def remote(n, src, dst, device):
        return pltpu.make_async_remote_copy(
            src_ref=src, dst_ref=dst, send_sem=ssem.at[n], recv_sem=rsem.at[n],
            device_id=device, device_id_type=MESH,
        )

    def send(n, src, dst, device):
        remote(n, src, dst, device).start()

    def arrived(n, dst):
        remote(n, dst, dst, at_y(1)).wait_recv()

    def sent(n, src):
        remote(n, src, src, at_y(1)).wait_send()

    peers = [at(d, 0) for d in range(1, nz)] + [at(0, d) for d in range(1, nx)]
    peers += [at_member(1, dx) for dx in range(1, nx)]
    peers += [at_y(d) for d in range(1, ny)] + ([sibling] if nc == 2 else [])
    for s in (0, REACH):
        kbuf[s] = jnp.zeros((nx, PACK, HEAD), bf16)
        vbuf[s] = jnp.zeros((keys, HEAD), bf16)
    barrier = pltpu.get_barrier_semaphore()
    for peer in peers:
        pl.semaphore_signal(barrier, inc=1, device_id=peer, device_id_type=MESH)

    mine = pl.ds(pl.multiple_of(x * TOK, TOK), TOK)
    local_in = [
        pltpu.make_async_copy(src, dst, lsem.at[n])
        for n, (src, dst) in enumerate([
            (k_ref.at[0], kbuf.at[0, x, 0:TOK]),
            (v_ref.at[0], vbuf.at[0, mine]),
            (q_ref.at[0], qin),
            (do_ref.at[0], doin),
            (o_ref.at[0], oin0),
            (w_ref, wf.at[y, c, lax.div(z, 2)]),
        ])
    ]
    for copy in local_in:
        copy.start()
    own_lab = lab_ref[...].astype(f32)
    kbuf[0, x, TOK:PACK] = jnp.broadcast_to(own_lab, (PACK - TOK, TOK)).astype(bf16)
    local_in[0].wait()
    local_in[1].wait()
    pl.semaphore_wait(barrier, len(peers))

    n_kz, n_vz = sems.take(planes), sems.take(planes)
    n_kx, n_vx = sems.take(planes * (nx - 1)), sems.take(planes * (nx - 1))

    def seen(s, key_x, query_x):
        inside = (s > 0) & (s < REACH)
        return inside | ((s == 0) & (key_x < query_x)) | ((s == REACH) & (key_x > query_x))

    def from_x(d):
        return lax.rem(x - d + nx, nx)

    def to_x(d):
        return lax.rem(x + d, nx)

    def keys_x(s):
        for d in range(1, nx):
            @pl.when(seen(s, x, to_x(d)))
            def _(d=d):
                send(n_kx + s * (nx - 1) + d - 1, kbuf.at[s, x], kbuf.at[s, x], at(0, d))

    def values_x(s):
        for d in range(1, nx):
            @pl.when(seen(s, x, to_x(d)))
            def _(d=d):
                send(n_vx + s * (nx - 1) + d - 1, vbuf.at[s, mine], vbuf.at[s, mine], at(0, d))

    n_kr, n_vr = sems.take(1), sems.take(1)
    send(n_kr, kbuf.at[0, x], krelay, at(-2, 0))
    for s in range(1, REACH):
        send(n_kz + s, kbuf.at[0, x], kbuf.at[s, x], at(s, 0))
    keys_x(0)

    far = [0, 2, -2, 4]
    n_w = sems.take(4)
    n_up, n_down = sems.take(4 * (half + 1)), sems.take(4 * (half + 1))
    n_over = sems.take(4 * (2 * half + 1))

    def share(head, k):
        return wf.at[head, c, lax.div(lax.rem(z + far[k] + nz, nz), 2)]

    def low(d):
        return lax.rem(y - d + ny, ny)

    def high(d):
        return lax.rem(y + d, ny)

    def over(k, d, up):
        return n_over + k * (2 * half + 1) + 2 * d - up

    def goes_up(k, d):
        return d < half or (d == half and k < 2)

    def goes_down(k, d):
        return d < half or (d == half and k >= 2)

    def w_start(k, source=None):
        source = share(y, k) if source is None else source
        send(n_up + k * (half + 1) + 1, source, share(y, k), at_y(1))
        send(n_down + k * (half + 1) + 1, source, share(y, k), at_y(-1))
        if nc == 2:
            send(over(k, 0, 0), source, share(y, k), sibling)

    passed = set()

    def w_pass(k, d):
        if (k, d) in passed:
            return
        passed.add((k, d))
        if goes_up(k, d):
            arrived(n_up + k * (half + 1) + d, share(low(d), k))
            if goes_up(k, d + 1):
                send(n_up + k * (half + 1) + d + 1, share(low(d), k), share(low(d), k), at_y(1))
            if nc == 2:
                send(over(k, d, 1), share(low(d), k), share(low(d), k), sibling)
        if goes_down(k, d):
            arrived(n_down + k * (half + 1) + d, share(high(d), k))
            if goes_down(k, d + 1):
                send(n_down + k * (half + 1) + d + 1, share(high(d), k), share(high(d), k), at_y(-1))
            if nc == 2:
                send(over(k, d, 0), share(high(d), k), share(high(d), k), sibling)

    w_start(0, w_ref)

    local_in[2].wait()
    for h in range(group):
        qs[h * TOK : (h + 1) * TOK, :] = qin[:, h * HEAD : (h + 1) * HEAD]

    for copy in local_in[3:]:
        copy.wait()
    lane = lax.broadcasted_iota(jnp.int32, (TOK, HEAD), 1)
    for h in range(group):
        cols = slice(h * HEAD, (h + 1) * HEAD)
        part = slice(h * TOK, (h + 1) * TOK)
        grad = doin[:, cols]
        dos[part, 0:HEAD] = grad
        delta = -jnp.sum(
            grad.astype(f32) * oin0[:, cols].astype(f32), axis=1, keepdims=True
        )
        first = delta.astype(bf16).astype(f32)
        second = (delta - first).astype(bf16).astype(f32)
        third = delta - first - second
        extra = jnp.where(lane == 0, first, jnp.where(lane == 1, second, third))
        dos[part, HEAD:] = jnp.where(lane < 3, extra, 0.0).astype(bf16)

    dqt[...] = jnp.zeros_like(dqt)
    row = lax.broadcasted_iota(jnp.int32, (TOK, TOK), 0)
    query_at = lane + ctx * TOK

    arrived(n_kr, krelay)
    send(n_kz + REACH, krelay, kbuf.at[REACH, x], at(-2, 0))
    for s in (2, 3, 1):
        send(n_vz + s, vbuf.at[0, mine], vbuf.at[s, mine], at(s, 0))
    send(n_vr, vbuf.at[0, mine], vrelay, at(-2, 0))
    for s in range(1, REACH):
        arrived(n_kz + s, kbuf.at[0, x])
        keys_x(s)
    values_x(0)
    send(n_w + 2, w_ref, share(y, 0), at(2, 0))
    send(n_w + 1, w_ref, share(y, 0), at(-2, 0))

    def pass_one(s, carry):
        @pl.when(s == 1)
        def _():
            arrived(n_kz + REACH, kbuf.at[0, x])
            keys_x(REACH)
            arrived(n_vr, vrelay)
            send(n_vz + REACH, vrelay, vbuf.at[REACH, mine], at(-2, 0))
            w_pass(0, 1)

        @pl.when(s == 2)
        def _():
            for n in (2, 3):
                arrived(n_vz + n, vbuf.at[0, mine])
                values_x(n)

        @pl.when(s == REACH)
        def _():
            for n in (REACH, 1):
                arrived(n_vz + n, vbuf.at[0, mine])
                values_x(n)
            arrived(n_w + 1, w_ref)
            send(n_w + 3, share(y, 1), share(y, 1), at(-2, 0))

        for d in range(1, nx):
            @pl.when(seen(s, from_x(d), x))
            def _(d=d):
                arrived(n_kx + s * (nx - 1) + d - 1, kbuf.at[0, x])

        plane = lax.rem(z - s + nz, nz)
        for other in range(nx):
            labels = kbuf[s, other, TOK:PACK].astype(f32)[0:1]
            labels = jnp.broadcast_to(labels, (TOK, TOK)).T
            key_at = row + (plane * nx + other) * TOK
            allowed = (labels == own_lab) & (key_at <= query_at)
            bias[other * TOK : (other + 1) * TOK, :] = jnp.where(allowed, 0.0, NEG)
        block = jnp.concatenate([kbuf[s, other, 0:TOK] for other in range(nx)], axis=0)
        width = 2 * TOK
        for i in range(wide // width):
            part = slice(i * width, (i + 1) * width)
            scores = dot(block, qs[part, :], NT) * (scale * LOG2E)
            more = bias[...]
            scores = scores + jnp.concatenate([more, more], axis=1)
            top = jnp.max(scores, axis=0, keepdims=True)
            e = jnp.exp2(scores - top)
            sbuf[s, :, part] = e
            mrow[s, :, part] = top
            lrow[s, :, part] = jnp.sum(e, axis=0, keepdims=True)

        return carry

    lax.fori_loop(0, planes, pass_one, 0)

    w_pass(0, 2)
    w_start(1)
    arrived(n_w + 2, w_ref)
    w_start(2)

    top = mrow[0]
    for s in range(1, planes):
        top = jnp.maximum(top, mrow[s])
    total = jnp.zeros_like(top)
    for s in range(planes):
        total = total + lrow[s] * jnp.exp2(mrow[s] - top)
    lse = top + jnp.log2(total)
    for s in range(planes):
        frow[s] = jnp.exp2(mrow[s] - lse)

    ones = jnp.where(
        lax.broadcasted_iota(jnp.int32, (keys, HEAD), 1) < 3, 1.0, 0.0
    ).astype(bf16)
    n_bx, n_bz = sems.take(planes * (nx - 1)), sems.take(planes)

    def summed(s):
        for d in range(1, nx):
            @pl.when(seen(s, x, from_x(d)))
            def _(d=d):
                arrived(n_bx + s * (nx - 1) + d - 1, rx.at[0, 0])

        total = own32[s]
        for d in range(nx - 1):
            got = rx[s, d].astype(f32)
            total = total + jnp.where(seen(s, x, from_x(d + 1)), got, 0.0)
        return total

    def plane_at(r):
        first = (REACH + 1 - r) // 3
        return first * (r + 2) + (1 - first) * (REACH - r)

    def back(s):
        zout[s] = summed(s).astype(bf16)
        send(n_bz + s, zout.at[s], rz.at[s], at(-s, 0))

    def pass_two(r, carry):
        s = plane_at(r)
        for d in range(1, nx):
            @pl.when(seen(s, from_x(d), x))
            def _(d=d):
                arrived(n_vx + s * (nx - 1) + d - 1, vbuf.at[0, mine])

        block = jnp.concatenate([kbuf[s, other, 0:TOK] for other in range(nx)], axis=0)
        kt[...] = block.astype(f32).T.astype(bf16)
        prob = sbuf[s] * frow[s]
        dprob = dot(jnp.concatenate([vbuf[s], ones], axis=1), dos[...], NT)
        dscore = (prob * dprob).astype(bf16)
        acc[:, HEAD:] = dot(prob.astype(bf16), dos[:, 0:HEAD], NN)
        acc[:, 0:HEAD] = dot(dscore, qs[...], NN) * scale
        dqt[...] += dot(kt[...], dscore, NN)
        for other in range(nx):
            outbox[s, other] = acc[other * TOK : (other + 1) * TOK, :].astype(bf16)
        own32[s] = acc[mine, :]
        for d in range(1, nx):
            @pl.when(seen(s, to_x(d), x))
            def _(d=d):
                send(
                    n_bx + s * (nx - 1) + d - 1,
                    outbox.at[s, to_x(d)], rx.at[s, d - 1], at(0, d),
                )

        @pl.when(r >= 2)
        def _():
            back(plane_at(r - 2))

        @pl.when(r == 1)
        def _():
            arrived(n_w + 3, w_ref)
            w_start(3)

        @pl.when(r == 2)
        def _():
            w_pass(1, 1)
            w_pass(2, 1)
            w_pass(0, 3)

        @pl.when(r == REACH)
        def _():
            w_pass(3, 1)
            w_pass(1, 2)
            w_pass(2, 2)

        return carry

    lax.fori_loop(0, planes, pass_two, 0)

    back(1)

    for h in range(group):
        cols = slice(h * HEAD, (h + 1) * HEAD)
        dq_out[0, :, cols] = (dqt[:, cols].T * scale).astype(bf16)
    local_out = [pltpu.make_async_copy(dq_out, dq_ref, lsem.at[6])]
    local_out[0].start()

    row_at = (row + ctx * TOK).astype(f32)
    angle = row_at * inv_ref[...]
    cosine, sine = jnp.cos(angle), jnp.sin(angle)

    total = summed(0)
    for s in range(1, planes):
        arrived(n_bz + s, rz.at[0])
        total = total + rz[s].astype(f32)
    key_sum = total[:, 0:HEAD]
    value_half = total[:, HEAD:].astype(bf16)
    turned = pltpu.roll(key_sum, HEAD // 2, axis=1)
    turned = jnp.where(lane < HEAD // 2, -turned, turned)
    gloc[:, 0:HEAD] = (key_sum * cosine - turned * sine).astype(bf16)
    gloc[:, HEAD:] = value_half

    n_gy, n_g, n_o = sems.take(ny), sems.take(len(members)), sems.take(2 * len(members))

    def tokens_of(d):
        return gloc.at[pl.ds(pl.multiple_of(lax.rem(y + d, ny) * piece, piece), piece)]

    for d in range(1, ny):
        send(n_gy + d, tokens_of(d), gy.at[y], at_y(d))
    gy[y] = gloc[pl.ds(pl.multiple_of(y * piece, piece), piece), :]
    dk_out[0] = key_sum.astype(bf16)
    dv_out[0] = value_half
    local_out.append(pltpu.make_async_copy(dk_out, dk_ref, lsem.at[7]))
    local_out.append(pltpu.make_async_copy(dv_out, dv_ref, lsem.at[8]))
    local_out[1].start()
    local_out[2].start()
    for k, d in ((0, 4), (3, 2), (1, 3), (2, 3)):
        w_pass(k, d)
    for d in range(1, ny):
        arrived(n_gy + d, gy.at[0])

    for n, (dp, dx) in enumerate(members):
        send(n_g + n, gy, gall.at[me], at_member(dp, dx))
    gall[me] = gy[...]
    w_pass(3, 3)
    for k in range(1, 4):
        w_pass(k, half)
    if nc == 2:
        for k in range(4):
            arrived(over(k, 0, 0), w_ref)
            for d in range(1, half + 1):
                if goes_up(k, d):
                    arrived(over(k, d, 1), w_ref)
                if goes_down(k, d):
                    arrived(over(k, d, 0), w_ref)
    for n in range(len(members)):
        arrived(n_g + n, gy)

    count = 2 * nx
    tokens = jnp.concatenate(
        [gall[:, h].reshape(count * piece, 2 * HEAD) for h in range(ny)], axis=1
    )
    side = lax.rem(x, 2)
    whole = pl.ds(pl.multiple_of(side * (HEAD // 2), HEAD // 2), HEAD)
    rest = pl.ds(pl.multiple_of((1 - side) * HEAD, HEAD // 2), HEAD // 2)

    def weight_rows(n, rows):
        core, j = n // slots, n % slots
        return jnp.concatenate([wf[h, core, j, rows, :] for h in range(ny)], axis=1)

    shares = nc * slots
    for n in range(0, shares, 2):
        block = jnp.concatenate([weight_rows(n, whole), weight_rows(n + 1, whole)], axis=0)
        part = dot(tokens, block, NT).astype(bf16)
        obuf[:, :, n * HEAD : (n + 2) * HEAD] = part.reshape(count, piece, 2 * HEAD)
    front = shares * HEAD
    lots = (pl.ds(0, front), pl.ds(front, front // 2))

    def hand_over(lot):
        for n, (dp, dx) in enumerate(members):
            send(
                n_o + 2 * n + lot, obuf.at[member(dp, dx), :, lots[lot]],
                oin.at[me, :, lots[lot]], at_member(dp, dx),
            )

    hand_over(0)
    for n in range(0, shares, 4):
        block = []
        for m in (n, n + 2):
            core, j = m // slots, m % slots
            first = jnp.concatenate([wf[h, core, j + side, rest, :] for h in range(ny)], axis=1)
            second = jnp.concatenate(
                [wf[h, core, j + 1 - side, rest, :] for h in range(ny)], axis=1
            )
            block += [first, second]
        part = dot(tokens, jnp.concatenate(block, axis=0), NT).astype(bf16)
        base = front + n * (HEAD // 2)
        obuf[:, :, base : base + 2 * HEAD] = part.reshape(count, piece, 2 * HEAD)

    hand_over(1)
    oin[me] = obuf[me]
    for n in range(len(members)):
        arrived(n_o + 2 * n, oin.at[0, :, lots[0]])
        arrived(n_o + 2 * n + 1, oin.at[0, :, lots[1]])
    left = lax.broadcasted_iota(jnp.int32, (piece, HEAD), 1) < HEAD // 2
    for p in range(2):
        for e in range(nx // 2):
            even, uneven = p * nx + 2 * e, p * nx + 2 * e + 1
            for n in range(shares):
                core, j = n // slots, n % slots
                first = core * (nz * nx * rb) + (2 * j + p) * nx * rb + e * 2 * rb
                dx_out[0, :, first : first + HEAD] = oin[even, :, n * HEAD : (n + 1) * HEAD]
                dx_out[0, :, first + 2 * HEAD : first + 3 * HEAD] = oin[
                    uneven, :, n * HEAD : (n + 1) * HEAD
                ]
                base = front + n // 2 * HEAD
                a = oin[even, :, base : base + HEAD].astype(f32)
                b = oin[uneven, :, base : base + HEAD].astype(f32)
                if n % 2 == 0:
                    middle = jnp.where(left, a, b)
                else:
                    middle = pltpu.roll(jnp.where(left, b, a), HEAD // 2, axis=1)
                dx_out[0, :, first + HEAD : first + 2 * HEAD] = middle.astype(bf16)
    local_out.append(pltpu.make_async_copy(dx_out, dx_ref, lsem.at[9]))
    local_out[3].start()

    for s in range(planes):
        for d in range(1, nx):
            @pl.when(seen(s, x, to_x(d)))
            def _(s=s, d=d):
                sent(n_kx + s * (nx - 1) + d - 1, kbuf.at[0, x])
                sent(n_vx + s * (nx - 1) + d - 1, vbuf.at[0, mine])

            @pl.when(seen(s, to_x(d), x))
            def _(s=s, d=d):
                sent(n_bx + s * (nx - 1) + d - 1, rx.at[0, 0])

        if s > 0:
            sent(n_kz + s, kbuf.at[0, x])
            sent(n_vz + s, vbuf.at[0, mine])
            sent(n_bz + s, rz.at[0])
    sent(n_kr, krelay)
    sent(n_vr, vrelay)
    for k in range(4):
        if k > 0:
            sent(n_w + k, w_ref)
        for d in range(1, half + 1):
            if goes_up(k, d):
                sent(n_up + k * (half + 1) + d, w_ref)
            if goes_down(k, d):
                sent(n_down + k * (half + 1) + d, w_ref)
            if nc == 2 and goes_up(k, d):
                sent(over(k, d, 1), w_ref)
            if nc == 2 and goes_down(k, d):
                sent(over(k, d, 0), w_ref)
        if nc == 2:
            sent(over(k, 0, 0), w_ref)
    for d in range(1, ny):
        sent(n_gy + d, gy.at[0])
    for n in range(len(members)):
        sent(n_g + n, gy)
        sent(n_o + 2 * n, oin.at[0, :, lots[0]])
        sent(n_o + 2 * n + 1, oin.at[0, :, lots[1]])
    for copy in local_out:
        copy.wait()


def hand_out(*refs):
    count = len(refs) // 3
    sources, targets, held, sem = refs[:count], refs[count : 2 * count], refs[2 * count : -1], refs[-1]
    into = [pltpu.make_async_copy(sources[n], held[n], sem.at[n]) for n in range(count)]
    out = [pltpu.make_async_copy(held[n], targets[n], sem.at[count + n]) for n in range(count)]
    for copy in into:
        copy.start()
    for n in range(count):
        into[n].wait()
        out[n].start()
    for copy in out:
        copy.wait()


def local(sizes, q, k, v, o, do, lab, w):
    nc, nz, nx, ny = sizes
    group = q.shape[-1] // HEAD
    rb = w.shape[0]
    planes, keys, piece = REACH + 1, nx * TOK, TOK // ny
    d_all = rb * nc * nz * nx
    half = HEAD // 2
    inv = np.exp(
        -np.log(np.float32(1000000.0)) * (np.float32(2.0) * np.arange(half, dtype=np.float32) / HEAD)
    ).astype(np.float32)
    inv = jnp.asarray(np.concatenate([inv, inv])[None, :])
    copies = 200
    vm = pltpu.VMEM
    wide = group * TOK
    share = nc * (nz // 2) * rb
    scratch = [
        vm((TOK, wide), bf16),
        vm((TOK, wide), bf16),
        vm((TOK, wide), bf16),
        vm((wide, HEAD), bf16),
        vm((wide, 2 * HEAD), bf16),
        vm((planes, nx, PACK, HEAD), bf16),
        vm((planes, keys, HEAD), bf16),
        vm((HEAD, keys), bf16),
        vm((planes, keys, wide), f32),
        vm((keys, TOK), f32),
        vm((planes, 1, wide), f32),
        vm((planes, 1, wide), f32),
        vm((planes, 1, wide), f32),
        vm((HEAD, wide), f32),
        vm((keys, 2 * HEAD), f32),
        vm((planes, nx, TOK, 2 * HEAD), bf16),
        vm((planes, TOK, 2 * HEAD), f32),
        vm((planes, nx - 1, TOK, 2 * HEAD), bf16),
        vm((planes, TOK, 2 * HEAD), bf16),
        vm((planes, TOK, 2 * HEAD), bf16),
        vm((TOK, 2 * HEAD), bf16),
        vm((ny, piece, 2 * HEAD), bf16),
        vm((2 * nx, ny, piece, 2 * HEAD), bf16),
        vm((2 * nx, piece, share), bf16),
        vm((2 * nx, piece, share), bf16),
        vm((ny, nc, nz // 2, rb, 2 * HEAD), bf16),
        vm((PACK, HEAD), bf16),
        vm((TOK, HEAD), bf16),
        vm(q.shape, bf16),
        vm(k.shape, bf16),
        vm(v.shape, bf16),
        vm((1, piece, d_all), bf16),
        pltpu.SemaphoreType.DMA((copies,)),
        pltpu.SemaphoreType.DMA((copies,)),
        pltpu.SemaphoreType.DMA((10,)),
    ]
    spec = pl.BlockSpec(memory_space=pltpu.VMEM)
    far = pl.BlockSpec(memory_space=pltpu.HBM)
    results = tuple(
        jax.ShapeDtypeStruct(shape, bf16)
        for shape in (q.shape, k.shape, v.shape, (1, piece, d_all))
    )
    out = pl.pallas_call(
        functools.partial(kernel, nc, nz, nx, ny, group, rb),
        out_shape=results,
        in_specs=[spec] * 2 + [far] * 6,
        out_specs=(far,) * 4,
        scratch_shapes=scratch,
        compiler_params=pltpu.CompilerParams(
            collective_id=0, has_side_effects=True, vmem_limit_bytes=60 * 1024 * 1024
        ),
    )(lab, inv, q, k, v, o, do, w)
    return pl.pallas_call(
        hand_out,
        out_shape=results,
        in_specs=[far] * 4,
        out_specs=(far,) * 4,
        scratch_shapes=[vm(r.shape, bf16) for r in results] + [pltpu.SemaphoreType.DMA((8,))],
    )(*out)


def solution(mesh):
    nx = NX
    sizes = (mesh.shape["dp"], mesh.shape["ctx"] // nx, nx, mesh.shape["tp"])
    in_specs = (
        P("dp", "ctx", "tp"),
        P("dp", "ctx", "tp"),
        P("dp", "ctx", "tp"),
        P("dp", "ctx", "tp"),
        P("dp", "ctx", "tp"),
        P("dp", "ctx"),
        P(("dp", "ctx"), "tp"),
    )
    out_specs = (
        P("dp", "ctx", "tp"),
        P("dp", "ctx", "tp"),
        P("dp", "ctx", "tp"),
        P("dp", ("ctx", "tp"), None),
    )
    return jax.shard_map(
        functools.partial(local, sizes),
        mesh=mesh, in_specs=in_specs, out_specs=out_specs, check_vma=False,
    )
```
